32 devices in a mesh: line: 4 (over z), bus: 4 (over y, core), tm: 2 (over x).
Axes of the slice: x: 2, y: 2, z: 4, core: 2. Of those that a mesh axis runs over, the one named last changes fastest.
Arguments:
- ptdf_matrix: float32 [15360, 12288], P('line', 'bus'), may hold values from -0.0546875 to 0.0546875
- bus_load: float32 [12288, 256], P('bus', 'tm'), may hold values from 0 to 1
- unit_bus: int32 [4096], P(('line', 'bus')), may hold values from 0 to 12287, as said below
- unit_type: int32 [4096], P(('line', 'bus')), may hold values from 0 to 3
- unit_limit: int32 [4096], P(('line', 'bus')), may hold values from 50 to 499
- unit_cost: float32 [4096], P(('line', 'bus')), may hold values from 0.1 to 1
- line_rating: int32 [15360], P('line'), may hold values from 20 to 299
Outputs:
- generation: float32 [4096, 256], P(('line', 'bus'), 'tm')
- line_dual: float32 [15360, 256], P('line', 'tm')
The draws below stay inside these ranges and needn't reach their ends.
Inputs may be any that keep to these rules, and one draw needn't show every extreme that they name: `unit_bus`: let G be the number of devices of line and bus together, U = 4096 / G and S = 12288 / G. Unit u lies in group q = u // U; it sits at a bus of the S consecutive buses that begin at (q mod the size of bus) * 12288 / (size of bus) + (q // size of bus) * S.
All inputs are finite; a program needn't handle non-finite values.
Results may differ from the reference program's by a relative error of at most 0.0003.
Values sent between devices are 32-bit elements; how exact they have to be, the bound alone decides.
A program may use at most 192 MiB of HBM per device.

```python
import math
import jax
import jax.numpy as jnp
from jax import lax

BUSES = 12288
LINES = 15360
UNITS = 4096
HOUR_DEV = 128
ITERS = 4
N_LINE = 4
N_BUS = 4
N_TM = 2


def draw_unit_bus(key, part):
    groups = N_LINE * N_BUS
    per_group = UNITS // groups
    sub_rows = BUSES // groups
    block_rows = BUSES // N_BUS
    owner = jnp.arange(UNITS, dtype=jnp.int32) // per_group
    line_place = owner // N_BUS
    bus_place = owner % N_BUS
    offset = jax.random.randint(key, (UNITS,), 0, sub_rows, dtype=jnp.int32)
    return (bus_place * block_rows + line_place * sub_rows + offset).astype(jnp.int32)


def draw_bus_load(key, part):
    key_profile = jax.random.fold_in(key, 11)
    key_local = jax.random.fold_in(key, 12)
    profile = jax.random.uniform(key_profile, (1, BUSES * 0 + HOUR_DEV * N_TM), jnp.float32, 0.1, 1.0)
    local = jax.random.uniform(key_local, (BUSES, HOUR_DEV * N_TM), jnp.float32, 0.3, 1.0)
    return (local * profile).astype(jnp.float32)


def place_ends(result, key, low, top_value):
    spot = [jax.random.randint(jax.random.fold_in(key, axis), (), 0, length) for axis, length in enumerate(result.shape)]
    main_axis = result.shape.index(max(result.shape))
    next_to = spot[:main_axis] + [(spot[main_axis] + 1) % result.shape[main_axis]] + spot[main_axis + 1:]
    return result.at[tuple(spot)].set(low).at[tuple(next_to)].set(top_value)


def steps_of(own_key, extent, pieces, low, largest):
    loudness, own = 1.0, jax.random.fold_in(own_key, 6)
    for position, blocks in pieces:
        steps = jnp.exp(jax.random.uniform(jax.random.fold_in(own, position), (blocks,), jnp.float32, low / len(pieces), largest / len(pieces)))
        loudness = loudness * jnp.repeat(steps, extent[position] // blocks).reshape([-1 if axis == position else 1 for axis in range(len(extent))])
    return loudness


def scatter_about(key, dims, deviation, most, shards=(), kind=jnp.bfloat16):
    level = steps_of(key, dims, shards, -0.22, 0.18) if shards else 1.0
    entries = jax.random.normal(key, dims, jnp.float32) * deviation * level
    return jnp.minimum(jnp.maximum(entries, -most), most).astype(kind)


def setup_inputs(seed: int = 0) -> dict:
    key_of = jax.random.split(jax.random.key(seed), 8)
    return {
        "ptdf_matrix": scatter_about(key_of[0], (LINES, BUSES), BUSES ** -0.5, 0.0546875, ((0, 4), (1, 4)), jnp.float32),
        "bus_load": draw_bus_load(jax.random.fold_in(key_of[7], 71), 0),
        "unit_bus": draw_unit_bus(jax.random.fold_in(key_of[7], 71), 0),
        "unit_type": place_ends(jax.random.randint(key_of[3], (UNITS,), 0, 4), jax.random.fold_in(key_of[3], 1), 0, 3).astype(jnp.int32),
        "unit_limit": place_ends(jax.random.randint(key_of[4], (UNITS,), 50, 500), jax.random.fold_in(key_of[4], 1), 50, 499).astype(jnp.int32),
        "unit_cost": jnp.clip(jnp.exp(math.log(1.0) - 2.3025851 * jax.random.uniform(key_of[5], (UNITS,), jnp.float32) ** steps_of(key_of[5], (UNITS,), ((0, 16),), -0.2, 0.2)), 0.1, 1.0),
        "line_rating": place_ends(jax.random.randint(key_of[6], (LINES,), 20, 300), jax.random.fold_in(key_of[6], 1), 20, 299).astype(jnp.int32),
    }


RAMP_RATES = (0.1, 0.2, 0.4, 0.5)
COST_FACTORS = (1.0, 1.5, 3.0, 0.05)
PRIMAL_STEP = 0.5
DUAL_STEP = 0.5


def unit_tables(unit_type, unit_limit, unit_cost):
    capacity = unit_limit.astype(jnp.float32) / 100.0
    kinds = (unit_type[:, None] == jnp.arange(4, dtype=jnp.int32)[None, :]).astype(jnp.float32)
    rates = jnp.sum(kinds * jnp.array(RAMP_RATES, jnp.float32)[None, :], axis=1)
    factors = jnp.sum(kinds * jnp.array(COST_FACTORS, jnp.float32)[None, :], axis=1)
    storage = kinds[:, 3]
    return unit_cost * factors, -capacity * storage, capacity, rates * capacity, storage, 2.0 * capacity


def reference(ptdf_matrix, bus_load, unit_bus, unit_type, unit_limit, unit_cost, line_rating):
    cost, lower_limit, upper_limit, ramp, storage, energy = unit_tables(unit_type, unit_limit, unit_cost)
    rating = (line_rating.astype(jnp.float32) / 100.0)[:, None]
    hour_count = bus_load.shape[1]
    hour_mask = (jnp.arange(hour_count) >= 1).astype(jnp.float32)[None, :]
    demand = jnp.sum(bus_load, axis=0)
    generation = jnp.zeros((UNITS, hour_count), jnp.float32)
    ramp_dual = jnp.zeros((UNITS, hour_count), jnp.float32)
    store_dual = jnp.zeros((UNITS, hour_count), jnp.float32)
    line_dual = jnp.zeros((LINES, hour_count), jnp.float32)
    balance_dual = jnp.zeros((hour_count,), jnp.float32)
    zero_column = jnp.zeros((UNITS, 1), jnp.float32)
    for iteration in range(ITERS):
        prices = jnp.dot(ptdf_matrix.T, line_dual, precision=lax.Precision.HIGHEST, preferred_element_type=jnp.float32)
        ramp_next = jnp.concatenate([ramp_dual[:, 1:], zero_column], axis=1)
        suffix = jnp.flip(jnp.cumsum(jnp.flip(store_dual, 1), axis=1), 1)
        gradient = cost[:, None] + balance_dual[None, :] + prices[unit_bus] + ramp_dual - ramp_next + storage[:, None] * suffix
        updated = jnp.clip(generation - PRIMAL_STEP * gradient, lower_limit[:, None], upper_limit[:, None])
        extrap = 2.0 * updated - generation
        injection = jax.ops.segment_sum(extrap, unit_bus, num_segments=BUSES) - bus_load
        flow = jnp.dot(ptdf_matrix, injection, precision=lax.Precision.HIGHEST, preferred_element_type=jnp.float32)
        moved = line_dual + DUAL_STEP * flow
        line_dual = moved - jnp.clip(moved, -DUAL_STEP * rating, DUAL_STEP * rating)
        balance_dual = balance_dual + (jnp.sum(extrap, axis=0) - demand) / UNITS
        previous = jnp.concatenate([zero_column, extrap[:, :-1]], axis=1)
        moved = ramp_dual + DUAL_STEP * (extrap - previous) * hour_mask
        ramp_dual = moved - jnp.clip(moved, -DUAL_STEP * ramp[:, None], DUAL_STEP * ramp[:, None])
        moved = store_dual + DUAL_STEP * storage[:, None] * jnp.cumsum(extrap, axis=1)
        store_dual = moved - jnp.clip(moved, -DUAL_STEP * energy[:, None], DUAL_STEP * energy[:, None])
        generation = updated
    return generation, line_dual
```

```python
import functools

import jax
import jax.numpy as jnp
from jax import lax
from jax.experimental import pallas as pl
from jax.experimental.pallas import tpu as pltpu
from jax.sharding import PartitionSpec as P

UNITS = 4096
ITERS = 4


RAMP_RATES = (0.1, 0.2, 0.4, 0.5)
COST_FACTORS = (1.0, 1.5, 3.0, 0.05)
PRIMAL_STEP = 0.5
DUAL_STEP = 0.5


def unit_tables(unit_type, unit_limit, unit_cost):
    capacity = unit_limit.astype(jnp.float32) / 100.0
    kinds = (unit_type[:, None] == jnp.arange(4, dtype=jnp.int32)[None, :]).astype(jnp.float32)
    rates = jnp.sum(kinds * jnp.array(RAMP_RATES, jnp.float32)[None, :], axis=1)
    factors = jnp.sum(kinds * jnp.array(COST_FACTORS, jnp.float32)[None, :], axis=1)
    storage = kinds[:, 3]
    return (
        unit_cost * factors,
        -capacity * storage,
        capacity,
        rates * capacity,
        storage,
        2.0 * capacity,
    )


def parts(value):
    high = lax.reduce_precision(value, 8, 7)
    return high.astype(jnp.bfloat16), (value - high).astype(jnp.bfloat16)


def exact(left, right):
    return jnp.dot(left, right, precision=lax.Precision.HIGHEST, preferred_element_type=jnp.float32)


def shifted(value, axis, by):
    length = lax.axis_size(axis)
    pairs = [(i, i + by) for i in range(length) if 0 <= i + by < length]
    return lax.ppermute(value, axis, pairs)


def gathered(edge, total, axis, sign):
    edge_there, total_there = jnp.zeros_like(edge), jnp.zeros_like(total)
    for k in range(1, lax.axis_size(axis)):
        if k == 1:
            both = shifted(jnp.stack([edge, total]), axis, sign)
            edge_there, total_there = both[0], both[1]
        else:
            total_there = total_there + shifted(total, axis, sign * k)
    return edge_there, total_there


def setup_kernel(groups, units, sub, ptdf_ref, pick_ref, load_ref, high_ref, low_ref, flow_ref):
    hours = flow_ref.shape[1]
    flow = jnp.zeros(flow_ref.shape, jnp.float32)
    for g in range(groups):
        tile = ptdf_ref[:, g * sub:(g + 1) * sub]
        high = tile.astype(jnp.bfloat16)
        low = (tile - high.astype(jnp.float32)).astype(jnp.bfloat16)
        pick = pick_ref[g * sub:(g + 1) * sub, :]
        load = load_ref[g * sub:(g + 1) * sub, :]
        own = slice(g * units, (g + 1) * units)
        high_ref[:, own] = jnp.dot(high, pick, preferred_element_type=jnp.float32).astype(jnp.bfloat16)
        low_ref[:, own] = jnp.dot(low, pick, preferred_element_type=jnp.float32).astype(jnp.bfloat16)
        wide = jnp.dot(high, load, preferred_element_type=jnp.float32)
        flow += wide[:, :hours] + wide[:, hours:]
        flow += jnp.dot(low, load[:, :hours], preferred_element_type=jnp.float32)
    flow_ref[...] = flow


def set_up(ptdf, pick, load, groups, units, sub):
    rows, buses = ptdf.shape
    hours = load.shape[1] // 2
    tile = next(t for t in (384, 256, 240, 192, 128, 64, 16) if rows % t == 0)
    chosen = groups * units
    return pl.pallas_call(
        functools.partial(setup_kernel, groups, units, sub),
        grid=(rows // tile,),
        in_specs=[
            pl.BlockSpec((tile, buses), lambda i: (i, 0)),
            pl.BlockSpec((buses, units), lambda i: (0, 0)),
            pl.BlockSpec((buses, 2 * hours), lambda i: (0, 0)),
        ],
        out_specs=[
            pl.BlockSpec((tile, chosen), lambda i: (i, 0)),
            pl.BlockSpec((tile, chosen), lambda i: (i, 0)),
            pl.BlockSpec((tile, hours), lambda i: (i, 0)),
        ],
        out_shape=[
            jax.ShapeDtypeStruct((rows, chosen), jnp.bfloat16),
            jax.ShapeDtypeStruct((rows, chosen), jnp.bfloat16),
            jax.ShapeDtypeStruct((rows, hours), jnp.float32),
        ],
        compiler_params=pltpu.CompilerParams(vmem_limit_bytes=48 * 1024 * 1024),
        cost_estimate=pl.CostEstimate(
            flops=4 * rows * buses * (units + 2 * hours),
            bytes_accessed=4 * rows * (buses + chosen + hours),
            transcendentals=0,
        ),
        name="unit_columns",
    )(ptdf, pick, load)


def on_device(ptdf_matrix, bus_load, unit_bus, unit_type, unit_limit, unit_cost, line_rating):
    line_place = lax.axis_index("line")
    bus_place = lax.axis_index("bus")
    tm_place = lax.axis_index("tm")
    groups = lax.axis_size("line")
    lines, block_rows = ptdf_matrix.shape
    sub = block_rows // groups
    hour_dev = bus_load.shape[1]
    units = unit_bus.shape[0]
    cost, lower_limit, upper_limit, ramp, storage, energy = unit_tables(
        unit_type, unit_limit, unit_cost
    )
    first = jnp.clip(-PRIMAL_STEP * cost, lower_limit, upper_limit)
    extrap_first = 2.0 * first
    place = (unit_bus - bus_place * block_rows - line_place * sub).astype(jnp.float32)
    both = lax.all_gather(jnp.stack([place, extrap_first]), "line", axis=0)
    places = both[:, 0].astype(jnp.int32)
    first_all = both[:, 1]
    pick = places[:, None, :] == jnp.arange(sub, dtype=jnp.int32)[None, :, None]
    placed = jnp.sum(jnp.where(pick, first_all[:, None, :], 0.0), axis=2).reshape(block_rows)
    pick = pick.astype(jnp.bfloat16).reshape(block_rows, units)
    injected = placed[:, None] - bus_load
    columns_high, columns_low, flow_first = set_up(
        ptdf_matrix, pick, jnp.concatenate(parts(injected), axis=1), groups, units, sub
    )
    rating = (line_rating.astype(jnp.float32) / 100.0)[:, None]
    earlier_index = jnp.arange(hour_dev, dtype=jnp.int32)[:, None]
    later_index = jnp.arange(hour_dev, dtype=jnp.int32)[None, :]
    forward_table = (earlier_index <= later_index).astype(jnp.float32)
    backward_table = (earlier_index >= later_index).astype(jnp.float32)
    hour_mask = (tm_place * hour_dev + jnp.arange(hour_dev, dtype=jnp.int32) >= 1).astype(
        jnp.float32
    )[None, :]
    load_total = jnp.sum(bus_load, axis=0)
    pad = 8

    generation = jnp.zeros((units, hour_dev), jnp.float32)
    ramp_dual = jnp.zeros((units, hour_dev), jnp.float32)
    store_dual = jnp.zeros((units, hour_dev), jnp.float32)
    balance_dual = jnp.zeros((hour_dev,), jnp.float32)
    line_dual = jnp.zeros((lines, hour_dev), jnp.float32)
    for iteration in range(ITERS):
        if iteration == 0:
            updated = jnp.broadcast_to(first[:, None], (units, hour_dev))
            extrap = 2.0 * updated
            flow_part = flow_first
            surplus_part = jnp.sum(first_all) - load_total
        else:
            dual_high, dual_low = parts(line_dual)
            over_lines = (((0,), (0,)), ((), ()))
            wide = lax.dot_general(
                columns_high,
                jnp.concatenate([dual_high, dual_low], axis=1),
                over_lines,
                preferred_element_type=jnp.float32,
            )
            narrow = lax.dot_general(
                columns_low, dual_high, over_lines, preferred_element_type=jnp.float32
            )
            unit_price = lax.psum_scatter(
                wide[:, :hour_dev] + wide[:, hour_dev:] + narrow,
                "line",
                scatter_dimension=0,
                tiled=True,
            )
            ramp_edge, store_after = gathered(
                ramp_dual[:, 0], jnp.sum(store_dual, axis=1), "tm", -1
            )
            ramp_next = jnp.concatenate([ramp_dual[:, 1:], ramp_edge[:, None]], axis=1)
            suffix = exact(store_dual, backward_table) + store_after[:, None]
            gradient = (
                cost[:, None]
                + balance_dual[None, :]
                + unit_price
                + ramp_dual
                - ramp_next
                + storage[:, None] * suffix
            )
            updated = jnp.clip(
                generation - PRIMAL_STEP * gradient, lower_limit[:, None], upper_limit[:, None]
            )
            extrap = 2.0 * updated - generation
            extrap_all = lax.all_gather(extrap, "line", axis=0, tiled=True)
            change = extrap_all - first_all.reshape(-1)[:, None]
            high, low = parts(change)
            wide = jnp.dot(
                columns_high,
                jnp.concatenate([high, low], axis=1),
                preferred_element_type=jnp.float32,
            )
            narrow = jnp.dot(columns_low, high, preferred_element_type=jnp.float32)
            flow_part = flow_first + wide[:, :hour_dev] + wide[:, hour_dev:] + narrow
            surplus_part = jnp.sum(extrap_all, axis=0) - load_total
        rows = jnp.concatenate(
            [flow_part, jnp.broadcast_to(surplus_part[None, :], (pad, hour_dev))], axis=0
        )
        total = lax.psum(rows, "bus")
        flow, surplus = total[:lines], total[lines]
        moved = line_dual + DUAL_STEP * flow
        line_dual = moved - jnp.clip(moved, -DUAL_STEP * rating, DUAL_STEP * rating)
        if iteration == ITERS - 1:
            return (updated, line_dual)
        balance_dual = balance_dual + surplus / UNITS
        prev_edge, store_before = gathered(extrap[:, -1], jnp.sum(extrap, axis=1), "tm", 1)
        previous = jnp.concatenate([prev_edge[:, None], extrap[:, :-1]], axis=1)
        moved = ramp_dual + DUAL_STEP * (extrap - previous) * hour_mask
        ramp_dual = moved - jnp.clip(moved, -DUAL_STEP * ramp[:, None], DUAL_STEP * ramp[:, None])
        running = exact(extrap, forward_table) + store_before[:, None]
        moved = store_dual + DUAL_STEP * storage[:, None] * running
        store_dual = moved - jnp.clip(
            moved, -DUAL_STEP * energy[:, None], DUAL_STEP * energy[:, None]
        )
        generation = updated


def solution(mesh):
    return jax.shard_map(
        on_device,
        mesh=mesh,
        in_specs=(
            P("line", "bus"),
            P("bus", "tm"),
            P(("line", "bus")),
            P(("line", "bus")),
            P(("line", "bus")),
            P(("line", "bus")),
            P("line"),
        ),
        out_specs=(P(("line", "bus"), "tm"), P("line", "tm")),
        check_vma=False,
    )
```

```python
import functools

import jax
import jax.numpy as jnp
from jax import lax
from jax.experimental import pallas as pl
from jax.experimental.pallas import tpu as pltpu
from jax.sharding import PartitionSpec as P

UNITS = 4096
ITERS = 4
MESH = pl.DeviceIdType.MESH


RAMP_RATES = (0.1, 0.2, 0.4, 0.5)
COST_FACTORS = (1.0, 1.5, 3.0, 0.05)
PRIMAL_STEP = 0.5
DUAL_STEP = 0.5


def unit_tables(unit_type, unit_limit, unit_cost):
    capacity = unit_limit.astype(jnp.float32) / 100.0
    kinds = (unit_type[:, None] == jnp.arange(4, dtype=jnp.int32)[None, :]).astype(jnp.float32)
    rates = jnp.sum(kinds * jnp.array(RAMP_RATES, jnp.float32)[None, :], axis=1)
    factors = jnp.sum(kinds * jnp.array(COST_FACTORS, jnp.float32)[None, :], axis=1)
    storage = kinds[:, 3]
    return (
        unit_cost * factors,
        -capacity * storage,
        capacity,
        rates * capacity,
        storage,
        2.0 * capacity,
    )


def parts(value):
    high = lax.reduce_precision(value, 8, 7)
    return high.astype(jnp.bfloat16), (value - high).astype(jnp.bfloat16)


def exact(left, right):
    return jnp.dot(left, right, precision=lax.Precision.HIGHEST, preferred_element_type=jnp.float32)


def shifted(value, axis, by):
    length = lax.axis_size(axis)
    pairs = [(i, i + by) for i in range(length) if 0 <= i + by < length]
    return lax.ppermute(value, axis, pairs)


def gathered(edge, total, axis, sign):
    edge_there, total_there = jnp.zeros_like(edge), jnp.zeros_like(total)
    for k in range(1, lax.axis_size(axis)):
        if k == 1:
            both = shifted(jnp.stack([edge, total]), axis, sign)
            edge_there, total_there = both[0], both[1]
        else:
            total_there = total_there + shifted(total, axis, sign * k)
    return edge_there, total_there


def setup_kernel(groups, units, sub, ptdf_ref, pick_ref, load_ref, high_ref, low_ref, flow_ref):
    hours = flow_ref.shape[1]
    flow = jnp.zeros(flow_ref.shape, jnp.float32)
    for g in range(groups):
        tile = ptdf_ref[:, g * sub:(g + 1) * sub]
        high = tile.astype(jnp.bfloat16)
        low = (tile - high.astype(jnp.float32)).astype(jnp.bfloat16)
        pick = pick_ref[g * sub:(g + 1) * sub, :]
        load = load_ref[g * sub:(g + 1) * sub, :]
        own = slice(g * units, (g + 1) * units)
        high_ref[:, own] = jnp.dot(high, pick, preferred_element_type=jnp.float32).astype(jnp.bfloat16)
        low_ref[:, own] = jnp.dot(low, pick, preferred_element_type=jnp.float32).astype(jnp.bfloat16)
        wide = jnp.dot(high, load, preferred_element_type=jnp.float32)
        flow += wide[:, :hours] + wide[:, hours:]
        flow += jnp.dot(low, load[:, :hours], preferred_element_type=jnp.float32)
    flow_ref[...] = flow


def set_up(ptdf, pick, load, groups, units, sub):
    rows, buses = ptdf.shape
    hours = load.shape[1] // 2
    tile = next(t for t in (384, 256, 240, 192, 128, 64, 16) if rows % t == 0)
    chosen = groups * units
    return pl.pallas_call(
        functools.partial(setup_kernel, groups, units, sub),
        grid=(rows // tile,),
        in_specs=[
            pl.BlockSpec((tile, buses), lambda i: (i, 0)),
            pl.BlockSpec((buses, units), lambda i: (0, 0)),
            pl.BlockSpec((buses, 2 * hours), lambda i: (0, 0)),
        ],
        out_specs=[
            pl.BlockSpec((tile, chosen), lambda i: (i, 0)),
            pl.BlockSpec((tile, chosen), lambda i: (i, 0)),
            pl.BlockSpec((tile, hours), lambda i: (i, 0)),
        ],
        out_shape=[
            jax.ShapeDtypeStruct((rows, chosen), jnp.bfloat16),
            jax.ShapeDtypeStruct((rows, chosen), jnp.bfloat16),
            jax.ShapeDtypeStruct((rows, hours), jnp.float32),
        ],
        compiler_params=pltpu.CompilerParams(vmem_limit_bytes=48 * 1024 * 1024),
        cost_estimate=pl.CostEstimate(
            flops=4 * rows * buses * (units + 2 * hours),
            bytes_accessed=4 * rows * (buses + chosen + hours),
            transcendentals=0,
        ),
        name="unit_columns",
    )(ptdf, pick, load)


def sum_kernel(part_ref, out_ref, there, chips, a_send, a_recv, b_send, b_recv, c_send, c_recv):
    bus = lax.axis_index("bus")
    chip_count = chips.shape[0]
    core, chip = lax.rem(bus, 2), lax.div(bus, 2)
    sibling = bus + 1 - 2 * core
    half = there.shape[0]
    spans = spans_of(half)
    mine, other = core * half, (1 - core) * half
    partners = [lax.rem(chip + j, chip_count) * 2 + core for j in range(1, chip_count)]

    barrier = pltpu.get_barrier_semaphore()
    for peer in [sibling] + partners:
        pl.semaphore_signal(barrier, inc=1, device_id={"bus": peer}, device_id_type=MESH)
    pl.semaphore_wait(barrier, 1 + len(partners))

    def rows(begin, span):
        return pl.ds(pl.multiple_of(begin + span[0], 8), span[1])

    def send(source, target, send_sem, recv_sem, peer):
        copy = pltpu.make_async_remote_copy(
            src_ref=source,
            dst_ref=target,
            send_sem=send_sem,
            recv_sem=recv_sem,
            device_id={"bus": peer},
            device_id_type=MESH,
        )
        copy.start()
        return copy

    halves = [
        send(part_ref.at[rows(other, span)], there.at[rows(0, span)], a_send.at[i], a_recv.at[i], sibling)
        for i, span in enumerate(spans)
    ]
    crossing = []
    for i, span in enumerate(spans):
        halves[i].wait_recv()
        chips[chip, rows(0, span), :] = part_ref[rows(mine, span), :] + there[rows(0, span), :]
        place = chips.at[chip, rows(0, span)]
        crossing.append(
            [
                send(place, place, b_send.at[j, i], b_recv.at[j, i], peer)
                for j, peer in enumerate(partners)
            ]
        )
    sums = []
    for i, span in enumerate(spans):
        for copy in crossing[i]:
            copy.wait_recv()
        total = chips[0, rows(0, span), :]
        for k in range(1, chip_count):
            total = total + chips[k, rows(0, span), :]
        out_ref[rows(mine, span), :] = total
        place = out_ref.at[rows(mine, span)]
        sums.append(send(place, place, c_send.at[i], c_recv.at[i], sibling))
    for i in range(len(spans)):
        sums[i].wait_recv()
    for i in range(len(spans)):
        halves[i].wait_send()
        for copy in crossing[i]:
            copy.wait_send()
        sums[i].wait_send()


def spans_of(half, count=6):
    tiles = half // 8
    ends = [8 * (tiles * i // count) for i in range(count + 1)]
    return [(a, b - a) for a, b in zip(ends[:-1], ends[1:]) if b > a]


def sum_over_bus(part):
    rows, hours = part.shape
    half, chip_count = rows // 2, lax.axis_size("bus") // 2
    spans = len(spans_of(half))
    one, many = pltpu.SemaphoreType.DMA((spans,)), pltpu.SemaphoreType.DMA((chip_count - 1, spans))
    return pl.pallas_call(
        sum_kernel,
        out_shape=jax.ShapeDtypeStruct(part.shape, part.dtype),
        in_specs=[pl.BlockSpec(memory_space=pltpu.VMEM)],
        out_specs=pl.BlockSpec(memory_space=pltpu.VMEM),
        scratch_shapes=[
            pltpu.VMEM((half, hours), part.dtype),
            pltpu.VMEM((chip_count, half, hours), part.dtype),
            one, one, many, many, one, one,
        ],
        compiler_params=pltpu.CompilerParams(
            collective_id=0, has_side_effects=True, vmem_limit_bytes=32 * 1024 * 1024
        ),
        cost_estimate=pl.CostEstimate(
            flops=2 * rows * hours, bytes_accessed=8 * rows * hours, transcendentals=0
        ),
        name="sum_over_bus",
    )(part)


def greet(axis):
    me, count = lax.axis_index(axis), lax.axis_size(axis)
    peers = [lax.rem(me + j, count) for j in range(1, count)]
    barrier = pltpu.get_barrier_semaphore()
    for peer in peers:
        pl.semaphore_signal(barrier, inc=1, device_id={axis: peer}, device_id_type=MESH)
    pl.semaphore_wait(barrier, count - 1)
    return me, peers


def gather_kernel(block_ref, out_ref, send_sem, recv_sem):
    me, peers = greet("line")
    own = out_ref.at[me]
    copies = [
        pltpu.make_async_remote_copy(
            src_ref=block_ref,
            dst_ref=own,
            send_sem=send_sem.at[j],
            recv_sem=recv_sem.at[j],
            device_id={"line": peer},
            device_id_type=MESH,
        )
        for j, peer in enumerate(peers)
    ]
    for copy in copies:
        copy.start()
    out_ref[me] = block_ref[...]
    for copy in copies:
        copy.wait_recv()
    for copy in copies:
        copy.wait_send()


def scatter_kernel(parts_ref, out_ref, slots, send_sem, recv_sem):
    me, peers = greet("line")
    copies = [
        pltpu.make_async_remote_copy(
            src_ref=parts_ref.at[peer],
            dst_ref=slots.at[j],
            send_sem=send_sem.at[j],
            recv_sem=recv_sem.at[j],
            device_id={"line": peer},
            device_id_type=MESH,
        )
        for j, peer in enumerate(peers)
    ]
    for copy in copies:
        copy.start()
    for copy in copies:
        copy.wait_recv()
    total = parts_ref[me]
    for j in range(len(peers)):
        total = total + slots[j]
    out_ref[...] = total
    for copy in copies:
        copy.wait_send()


def line_call(kernel, value, shape, slots, ident, name):
    sems = pltpu.SemaphoreType.DMA((lax.axis_size("line") - 1,))
    return pl.pallas_call(
        kernel,
        out_shape=jax.ShapeDtypeStruct(shape, value.dtype),
        in_specs=[pl.BlockSpec(memory_space=pltpu.VMEM)],
        out_specs=pl.BlockSpec(memory_space=pltpu.VMEM),
        scratch_shapes=slots + [sems, sems],
        compiler_params=pltpu.CompilerParams(
            collective_id=ident, has_side_effects=True, vmem_limit_bytes=32 * 1024 * 1024
        ),
        name=name,
    )(value)


def gather_line(value, ident):
    shape = (lax.axis_size("line"),) + value.shape
    return line_call(gather_kernel, value, shape, [], ident, "gather_line")


def scatter_line(value, ident):
    count = lax.axis_size("line")
    shape = (value.shape[0] // count,) + value.shape[1:]
    slots = [pltpu.VMEM((count - 1,) + shape, value.dtype)]
    return line_call(
        scatter_kernel, value.reshape((count,) + shape), shape, slots, ident, "scatter_line"
    )


def on_device(ptdf_matrix, bus_load, unit_bus, unit_type, unit_limit, unit_cost, line_rating):
    line_place = lax.axis_index("line")
    bus_place = lax.axis_index("bus")
    tm_place = lax.axis_index("tm")
    groups = lax.axis_size("line")
    lines, block_rows = ptdf_matrix.shape
    sub = block_rows // groups
    hour_dev = bus_load.shape[1]
    units = unit_bus.shape[0]
    cost, lower_limit, upper_limit, ramp, storage, energy = unit_tables(
        unit_type, unit_limit, unit_cost
    )
    first = jnp.clip(-PRIMAL_STEP * cost, lower_limit, upper_limit)
    extrap_first = 2.0 * first
    place = (unit_bus - bus_place * block_rows - line_place * sub).astype(jnp.float32)
    both = gather_line(jnp.stack([place, extrap_first] * 4), 1)
    places = both[:, 0].astype(jnp.int32)
    first_all = both[:, 1]
    pick = places[:, None, :] == jnp.arange(sub, dtype=jnp.int32)[None, :, None]
    placed = jnp.sum(jnp.where(pick, first_all[:, None, :], 0.0), axis=2).reshape(block_rows)
    pick = pick.astype(jnp.bfloat16).reshape(block_rows, units)
    injected = placed[:, None] - bus_load
    columns_high, columns_low, flow_first = set_up(
        ptdf_matrix, pick, jnp.concatenate(parts(injected), axis=1), groups, units, sub
    )
    rating = (line_rating.astype(jnp.float32) / 100.0)[:, None]
    earlier_index = jnp.arange(hour_dev, dtype=jnp.int32)[:, None]
    later_index = jnp.arange(hour_dev, dtype=jnp.int32)[None, :]
    forward_table = (earlier_index <= later_index).astype(jnp.float32)
    backward_table = (earlier_index >= later_index).astype(jnp.float32)
    hour_mask = (tm_place * hour_dev + jnp.arange(hour_dev, dtype=jnp.int32) >= 1).astype(
        jnp.float32
    )[None, :]
    load_total = jnp.sum(bus_load, axis=0)
    pad = 16

    generation = jnp.zeros((units, hour_dev), jnp.float32)
    ramp_dual = jnp.zeros((units, hour_dev), jnp.float32)
    store_dual = jnp.zeros((units, hour_dev), jnp.float32)
    balance_dual = jnp.zeros((hour_dev,), jnp.float32)
    line_dual = jnp.zeros((lines, hour_dev), jnp.float32)
    for iteration in range(ITERS):
        if iteration == 0:
            updated = jnp.broadcast_to(first[:, None], (units, hour_dev))
            extrap = 2.0 * updated
            flow_part = flow_first
            surplus_part = jnp.sum(first_all) - load_total
        else:
            dual_high, dual_low = parts(line_dual)
            over_lines = (((0,), (0,)), ((), ()))
            wide = lax.dot_general(
                columns_high,
                jnp.concatenate([dual_high, dual_low], axis=1),
                over_lines,
                preferred_element_type=jnp.float32,
            )
            narrow = lax.dot_general(
                columns_low, dual_high, over_lines, preferred_element_type=jnp.float32
            )
            unit_price = scatter_line(wide[:, :hour_dev] + wide[:, hour_dev:] + narrow, 3)
            ramp_edge, store_after = gathered(
                ramp_dual[:, 0], jnp.sum(store_dual, axis=1), "tm", -1
            )
            ramp_next = jnp.concatenate([ramp_dual[:, 1:], ramp_edge[:, None]], axis=1)
            suffix = exact(store_dual, backward_table) + store_after[:, None]
            gradient = (
                cost[:, None]
                + balance_dual[None, :]
                + unit_price
                + ramp_dual
                - ramp_next
                + storage[:, None] * suffix
            )
            updated = jnp.clip(
                generation - PRIMAL_STEP * gradient, lower_limit[:, None], upper_limit[:, None]
            )
            extrap = 2.0 * updated - generation
            extrap_all = gather_line(extrap, 2).reshape(-1, hour_dev)
            change = extrap_all - first_all.reshape(-1)[:, None]
            high, low = parts(change)
            wide = jnp.dot(
                columns_high,
                jnp.concatenate([high, low], axis=1),
                preferred_element_type=jnp.float32,
            )
            narrow = jnp.dot(columns_low, high, preferred_element_type=jnp.float32)
            flow_part = flow_first + wide[:, :hour_dev] + wide[:, hour_dev:] + narrow
            surplus_part = jnp.sum(extrap_all, axis=0) - load_total
        rows = jnp.concatenate(
            [flow_part, jnp.broadcast_to(surplus_part[None, :], (pad, hour_dev))], axis=0
        )
        total = sum_over_bus(rows)
        flow, surplus = total[:lines], total[lines]
        moved = line_dual + DUAL_STEP * flow
        line_dual = moved - jnp.clip(moved, -DUAL_STEP * rating, DUAL_STEP * rating)
        if iteration == ITERS - 1:
            return (updated, line_dual)
        balance_dual = balance_dual + surplus / UNITS
        prev_edge, store_before = gathered(extrap[:, -1], jnp.sum(extrap, axis=1), "tm", 1)
        previous = jnp.concatenate([prev_edge[:, None], extrap[:, :-1]], axis=1)
        moved = ramp_dual + DUAL_STEP * (extrap - previous) * hour_mask
        ramp_dual = moved - jnp.clip(moved, -DUAL_STEP * ramp[:, None], DUAL_STEP * ramp[:, None])
        running = exact(extrap, forward_table) + store_before[:, None]
        moved = store_dual + DUAL_STEP * storage[:, None] * running
        store_dual = moved - jnp.clip(
            moved, -DUAL_STEP * energy[:, None], DUAL_STEP * energy[:, None]
        )
        generation = updated


def solution(mesh):
    return jax.shard_map(
        on_device,
        mesh=mesh,
        in_specs=(
            P("line", "bus"),
            P("bus", "tm"),
            P(("line", "bus")),
            P(("line", "bus")),
            P(("line", "bus")),
            P(("line", "bus")),
            P("line"),
        ),
        out_specs=(P(("line", "bus"), "tm"), P("line", "tm")),
        check_vma=False,
    )
```

```python
import functools

import jax
import jax.numpy as jnp
from jax import lax
from jax.experimental import pallas as pl
from jax.experimental.pallas import tpu as pltpu
from jax.sharding import PartitionSpec as P

UNITS = 4096
ITERS = 4
MESH = pl.DeviceIdType.MESH


RAMP_RATES = (0.1, 0.2, 0.4, 0.5)
COST_FACTORS = (1.0, 1.5, 3.0, 0.05)
PRIMAL_STEP = 0.5
DUAL_STEP = 0.5


def unit_tables(unit_type, unit_limit, unit_cost):
    capacity = unit_limit.astype(jnp.float32) / 100.0
    kinds = (unit_type[:, None] == jnp.arange(4, dtype=jnp.int32)[None, :]).astype(jnp.float32)
    rates = jnp.sum(kinds * jnp.array(RAMP_RATES, jnp.float32)[None, :], axis=1)
    factors = jnp.sum(kinds * jnp.array(COST_FACTORS, jnp.float32)[None, :], axis=1)
    storage = kinds[:, 3]
    return (
        unit_cost * factors,
        -capacity * storage,
        capacity,
        rates * capacity,
        storage,
        2.0 * capacity,
    )


def parts(value):
    high = lax.reduce_precision(value, 8, 7)
    return high.astype(jnp.bfloat16), (value - high).astype(jnp.bfloat16)


def exact(left, right):
    return jnp.dot(left, right, precision=lax.Precision.HIGHEST, preferred_element_type=jnp.float32)


def shifted(value, axis, by):
    length = lax.axis_size(axis)
    pairs = [(i, i + by) for i in range(length) if 0 <= i + by < length]
    return lax.ppermute(value, axis, pairs)


def gathered(edge, total, axis, sign):
    edge_there, total_there = jnp.zeros_like(edge), jnp.zeros_like(total)
    for k in range(1, lax.axis_size(axis)):
        if k == 1:
            both = shifted(jnp.stack([edge, total]), axis, sign)
            edge_there, total_there = both[0], both[1]
        else:
            total_there = total_there + shifted(total, axis, sign * k)
    return edge_there, total_there


def stages(steps, tile, part, there, chips, done, sems):
    a_send, a_recv, b_send, b_recv, c_send, c_recv = sems
    bus = lax.axis_index("bus")
    chip_count = chips.shape[0]
    core, chip = lax.rem(bus, 2), lax.div(bus, 2)
    sibling = bus + 1 - 2 * core
    pairs = steps // 2
    half = pairs * tile
    mine, other = core * half, (1 - core) * half
    partners = [lax.rem(chip + j, chip_count) * 2 + core for j in range(1, chip_count)]

    def rows(begin, size):
        return pl.ds(pl.multiple_of(begin, 8), size)

    def copy(source, target, send_sem, recv_sem, peer):
        return pltpu.make_async_remote_copy(
            src_ref=source,
            dst_ref=target,
            send_sem=send_sem,
            recv_sem=recv_sem,
            device_id={"bus": peer},
            device_id_type=MESH,
        )

    def size_of(k):
        return 8 if isinstance(k, int) and k == pairs else tile

    def first(k):
        begin = 2 * half if isinstance(k, int) and k == pairs else other + k * tile
        return copy(
            part.at[rows(begin, size_of(k))],
            there.at[rows(k * tile, size_of(k))],
            a_send.at[k], a_recv.at[k], sibling,
        )

    def cross(k):
        place = chips.at[chip, rows(k * tile, size_of(k))]
        return [
            copy(place, place, b_send.at[j, k], b_recv.at[j, k], peer)
            for j, peer in enumerate(partners)
        ]

    def last(k):
        place = done.at[rows(mine + k * tile, tile)]
        return copy(place, place, c_send.at[k], c_recv.at[k], sibling)

    def enter():
        barrier = pltpu.get_barrier_semaphore()
        for peer in [sibling] + partners:
            pl.semaphore_signal(barrier, inc=1, device_id={"bus": peer}, device_id_type=MESH)
        pl.semaphore_wait(barrier, 1 + len(partners))

    def halve(k):
        first(k).wait_recv()
        begin = 2 * half if isinstance(k, int) and k == pairs else mine + k * tile
        here = rows(k * tile, size_of(k))
        chips[chip, here, :] = part[rows(begin, size_of(k)), :] + there[here, :]
        for each in cross(k):
            each.start()

    def total(k):
        for each in cross(k):
            each.wait_recv()
        here = rows(k * tile, size_of(k))
        value = chips[0, here, :]
        for c in range(1, chip_count):
            value = value + chips[c, here, :]
        return value

    def end():
        for k in range(pairs + 1):
            first(k).wait_send()
            for each in cross(k):
                each.wait_send()
        for k in range(pairs):
            last(k).wait_send()

    return enter, first, halve, total, last, end, rows, mine, other


def run_stages(steps, tile, make_tile, update, extra_ref, extra_out, part, there, chips, done, sems):
    enter, first, halve, total, last, end, rows, mine, other = stages(
        steps, tile, part, there, chips, done, sems
    )
    i = pl.program_id(0)
    pairs = steps // 2
    half = pairs * tile
    k = i // 2

    @pl.when(i == 0)
    def _():
        enter()
        part[2 * half:2 * half + 8, :] = extra_ref[...]
        first(pairs).start()

    part[rows((i % 2) * half + k * tile, tile), :] = make_tile()

    @pl.when(i == 1)
    def _():
        halve(pairs)

    @pl.when(i % 2 == 1)
    def _():
        first(k).start()

        @pl.when(k >= 1)
        def _():
            halve(k - 1)

    @pl.when(i == steps - 1)
    def _():
        halve(pairs - 1)
        for c in range(pairs):
            here = rows(mine + c * tile, tile)
            done[here, :] = total(c)
            last(c).start()
            update(here)
        extra_out[...] = total(pairs)
        for c in range(pairs):
            last(c).wait_recv()
            update(rows(other + c * tile, tile))
        end()


def store_dual_parts(moved, rating, here, dual_out, cat_out):
    hours = moved.shape[1]
    bound = DUAL_STEP * rating
    dual = moved - jnp.clip(moved, -bound, bound)
    high = dual.astype(jnp.bfloat16)
    dual_out[here, :] = dual
    cat_out[here, :hours] = high
    cat_out[here, hours:] = (dual - high.astype(jnp.float32)).astype(jnp.bfloat16)


def setup_kernel(
    groups, units, sub, steps, tile,
    ptdf_ref, pick_ref, load_ref, rating_ref, extra_ref,
    high_ref, low_ref, flow_out, dual_out, cat_out, extra_out,
    part, there, chips, done, *sems,
):
    hours = part.shape[1]

    def make_tile():
        flow = jnp.zeros((tile, hours), jnp.float32)
        for g in range(groups):
            block = ptdf_ref[:, g * sub:(g + 1) * sub]
            high = block.astype(jnp.bfloat16)
            low = (block - high.astype(jnp.float32)).astype(jnp.bfloat16)
            pick = pick_ref[g * sub:(g + 1) * sub, :]
            load = load_ref[g * sub:(g + 1) * sub, :]
            own = slice(g * units, (g + 1) * units)
            high_ref[:, own] = jnp.dot(
                high, pick, preferred_element_type=jnp.float32
            ).astype(jnp.bfloat16)
            low_ref[:, own] = jnp.dot(
                low, pick, preferred_element_type=jnp.float32
            ).astype(jnp.bfloat16)
            wide = jnp.dot(high, load, preferred_element_type=jnp.float32)
            flow += wide[:, :hours] + wide[:, hours:]
            flow += jnp.dot(low, load[:, :hours], preferred_element_type=jnp.float32)
        return flow

    def update(here):
        flow = done[here, :]
        flow_out[here, :] = flow
        store_dual_parts(DUAL_STEP * flow, rating_ref[here, :], here, dual_out, cat_out)

    run_stages(
        steps, tile, make_tile, update, extra_ref, extra_out, part, there, chips, done, sems
    )


def flow_kernel(
    steps, tile,
    high_ref, low_ref, change_ref, rating_ref, flow_ref, dual_ref, extra_ref,
    dual_out, cat_out, extra_out,
    part, there, chips, done, *sems,
):
    hours = part.shape[1]

    def make_tile():
        wide = jnp.dot(high_ref[...], change_ref[...], preferred_element_type=jnp.float32)
        narrow = jnp.dot(
            low_ref[...], change_ref[:, :hours], preferred_element_type=jnp.float32
        )
        return wide[:, :hours] + wide[:, hours:] + narrow

    def update(here):
        moved = dual_ref[here, :] + DUAL_STEP * (flow_ref[here, :] + done[here, :])
        store_dual_parts(moved, rating_ref[here, :], here, dual_out, cat_out)

    run_stages(
        steps, tile, make_tile, update, extra_ref, extra_out, part, there, chips, done, sems
    )


def tiles_of(lines):
    half = lines // 2
    sizes = (384, 320, 240, 192, 160, 128, 96, 64, 48, 32, 16)
    tile = next(t for t in sizes if half % t == 0)
    return 2 * (half // tile), tile


def whole(shape):
    return pl.BlockSpec(shape, lambda i: (0, 0), pipeline_mode=pl.Buffered(1))


def flow_scratch(lines, hours, steps):
    chip_count, pairs = lax.axis_size("bus") // 2, steps // 2
    first = pltpu.SemaphoreType.DMA((pairs + 1,))
    many = pltpu.SemaphoreType.DMA((chip_count - 1, pairs + 1))
    last = pltpu.SemaphoreType.DMA((pairs,))
    return [
        pltpu.VMEM((lines + 8, hours), jnp.float32),
        pltpu.VMEM((lines // 2 + 8, hours), jnp.float32),
        pltpu.VMEM((chip_count, lines // 2 + 8, hours), jnp.float32),
        pltpu.VMEM((lines, hours), jnp.float32),
        first, first, many, many, last, last,
    ]


def set_up(ptdf, pick, load, rating, extra, groups, units, sub):
    lines, buses = ptdf.shape
    hours = rating.shape[1]
    steps, tile = tiles_of(lines)
    chosen = groups * units
    pairs = steps // 2

    def order(i):
        return ((i % 2) * pairs + i // 2, 0)

    full = whole((lines, hours))
    return pl.pallas_call(
        functools.partial(setup_kernel, groups, units, sub, steps, tile),
        grid=(steps,),
        in_specs=[
            pl.BlockSpec((tile, buses), order),
            whole((buses, units)),
            whole((buses, 2 * hours)),
            full,
            whole((8, hours)),
        ],
        out_specs=[
            pl.BlockSpec((tile, chosen), order),
            pl.BlockSpec((tile, chosen), order),
            full,
            full,
            whole((lines, 2 * hours)),
            whole((8, hours)),
        ],
        out_shape=[
            jax.ShapeDtypeStruct((lines, chosen), jnp.bfloat16),
            jax.ShapeDtypeStruct((lines, chosen), jnp.bfloat16),
            jax.ShapeDtypeStruct((lines, hours), jnp.float32),
            jax.ShapeDtypeStruct((lines, hours), jnp.float32),
            jax.ShapeDtypeStruct((lines, 2 * hours), jnp.bfloat16),
            jax.ShapeDtypeStruct((8, hours), jnp.float32),
        ],
        scratch_shapes=flow_scratch(lines, hours, steps),
        compiler_params=pltpu.CompilerParams(
            collective_id=0, has_side_effects=True, vmem_limit_bytes=52 * 1024 * 1024
        ),
        cost_estimate=pl.CostEstimate(
            flops=4 * lines * buses * (units + 2 * hours),
            bytes_accessed=4 * lines * (buses + chosen + hours),
            transcendentals=0,
        ),
        name="first_flow",
    )(ptdf, pick, load, rating, extra)


def flow_step(high, low, change, rating, flow_first, dual, extra):
    lines, chosen = high.shape
    hours = dual.shape[1]
    steps, tile = tiles_of(lines)
    pairs = steps // 2

    def order(i):
        return ((i % 2) * pairs + i // 2, 0)

    full = whole((lines, hours))
    return pl.pallas_call(
        functools.partial(flow_kernel, steps, tile),
        grid=(steps,),
        in_specs=[
            pl.BlockSpec((tile, chosen), order),
            pl.BlockSpec((tile, chosen), order),
            whole((chosen, 2 * hours)),
            full,
            full,
            full,
            whole((8, hours)),
        ],
        out_specs=[full, whole((lines, 2 * hours)), whole((8, hours))],
        out_shape=[
            jax.ShapeDtypeStruct((lines, hours), jnp.float32),
            jax.ShapeDtypeStruct((lines, 2 * hours), jnp.bfloat16),
            jax.ShapeDtypeStruct((8, hours), jnp.float32),
        ],
        scratch_shapes=flow_scratch(lines, hours, steps),
        compiler_params=pltpu.CompilerParams(
            collective_id=4, has_side_effects=True, vmem_limit_bytes=44 * 1024 * 1024
        ),
        cost_estimate=pl.CostEstimate(
            flops=6 * lines * chosen * hours,
            bytes_accessed=4 * lines * (chosen + 6 * hours),
            transcendentals=0,
        ),
        name="flow_step",
    )(high, low, change, rating, flow_first, dual, extra)


def greet(axis):
    me, count = lax.axis_index(axis), lax.axis_size(axis)
    peers = [lax.rem(me + j, count) for j in range(1, count)]
    barrier = pltpu.get_barrier_semaphore()
    for peer in peers:
        pl.semaphore_signal(barrier, inc=1, device_id={axis: peer}, device_id_type=MESH)
    pl.semaphore_wait(barrier, count - 1)
    return me, peers


def gather_kernel(block_ref, out_ref, send_sem, recv_sem):
    me, peers = greet("line")
    own = out_ref.at[me]
    copies = [
        pltpu.make_async_remote_copy(
            src_ref=block_ref,
            dst_ref=own,
            send_sem=send_sem.at[j],
            recv_sem=recv_sem.at[j],
            device_id={"line": peer},
            device_id_type=MESH,
        )
        for j, peer in enumerate(peers)
    ]
    for copy in copies:
        copy.start()
    out_ref[me] = block_ref[...]
    for copy in copies:
        copy.wait_recv()
    for copy in copies:
        copy.wait_send()


def scatter_kernel(parts_ref, out_ref, slots, send_sem, recv_sem):
    me, peers = greet("line")
    copies = [
        pltpu.make_async_remote_copy(
            src_ref=parts_ref.at[peer],
            dst_ref=slots.at[j],
            send_sem=send_sem.at[j],
            recv_sem=recv_sem.at[j],
            device_id={"line": peer},
            device_id_type=MESH,
        )
        for j, peer in enumerate(peers)
    ]
    for copy in copies:
        copy.start()
    for copy in copies:
        copy.wait_recv()
    total = parts_ref[me]
    for j in range(len(peers)):
        total = total + slots[j]
    out_ref[...] = total
    for copy in copies:
        copy.wait_send()


def line_call(kernel, value, shape, slots, ident, name):
    sems = pltpu.SemaphoreType.DMA((lax.axis_size("line") - 1,))
    return pl.pallas_call(
        kernel,
        out_shape=jax.ShapeDtypeStruct(shape, value.dtype),
        in_specs=[pl.BlockSpec(memory_space=pltpu.VMEM)],
        out_specs=pl.BlockSpec(memory_space=pltpu.VMEM),
        scratch_shapes=slots + [sems, sems],
        compiler_params=pltpu.CompilerParams(
            collective_id=ident, has_side_effects=True, vmem_limit_bytes=32 * 1024 * 1024
        ),
        name=name,
    )(value)


def gather_line(value, ident):
    shape = (lax.axis_size("line"),) + value.shape
    return line_call(gather_kernel, value, shape, [], ident, "gather_line")


def scatter_line(value, ident):
    count = lax.axis_size("line")
    shape = (value.shape[0] // count,) + value.shape[1:]
    slots = [pltpu.VMEM((count - 1,) + shape, value.dtype)]
    return line_call(
        scatter_kernel, value.reshape((count,) + shape), shape, slots, ident, "scatter_line"
    )


def on_device(ptdf_matrix, bus_load, unit_bus, unit_type, unit_limit, unit_cost, line_rating):
    line_place = lax.axis_index("line")
    bus_place = lax.axis_index("bus")
    tm_place = lax.axis_index("tm")
    groups = lax.axis_size("line")
    lines, block_rows = ptdf_matrix.shape
    sub = block_rows // groups
    hour_dev = bus_load.shape[1]
    units = unit_bus.shape[0]
    cost, lower_limit, upper_limit, ramp, storage, energy = unit_tables(
        unit_type, unit_limit, unit_cost
    )
    first = jnp.clip(-PRIMAL_STEP * cost, lower_limit, upper_limit)
    extrap_first = 2.0 * first
    place = (unit_bus - bus_place * block_rows - line_place * sub).astype(jnp.float32)
    both = gather_line(jnp.stack([place, extrap_first] * 4), 1)
    places = both[:, 0].astype(jnp.int32)
    first_all = both[:, 1]
    pick = places[:, None, :] == jnp.arange(sub, dtype=jnp.int32)[None, :, None]
    placed = jnp.sum(jnp.where(pick, first_all[:, None, :], 0.0), axis=2).reshape(block_rows)
    pick = pick.astype(jnp.bfloat16).reshape(block_rows, units)
    injected = placed[:, None] - bus_load
    rating = jnp.broadcast_to(
        (line_rating.astype(jnp.float32) / 100.0)[:, None], (lines, hour_dev)
    )
    load_total = jnp.sum(bus_load, axis=0)

    def eight(surplus):
        return jnp.broadcast_to(surplus[None, :], (8, hour_dev))

    columns_high, columns_low, flow_first, line_dual, dual_cat, surplus = set_up(
        ptdf_matrix,
        pick,
        jnp.concatenate(parts(injected), axis=1),
        rating,
        eight(jnp.sum(first_all) - load_total),
        groups,
        units,
        sub,
    )
    earlier_index = jnp.arange(hour_dev, dtype=jnp.int32)[:, None]
    later_index = jnp.arange(hour_dev, dtype=jnp.int32)[None, :]
    forward_table = (earlier_index <= later_index).astype(jnp.float32)
    backward_table = (earlier_index >= later_index).astype(jnp.float32)
    hour_mask = (tm_place * hour_dev + jnp.arange(hour_dev, dtype=jnp.int32) >= 1).astype(
        jnp.float32
    )[None, :]
    generation = jnp.zeros((units, hour_dev), jnp.float32)
    ramp_dual = jnp.zeros((units, hour_dev), jnp.float32)
    store_dual = jnp.zeros((units, hour_dev), jnp.float32)
    balance_dual = jnp.zeros((hour_dev,), jnp.float32)
    for iteration in range(ITERS):
        if iteration == 0:
            updated = jnp.broadcast_to(first[:, None], (units, hour_dev))
            extrap = 2.0 * updated
            prev_edge = jnp.where(tm_place > 0, extrap_first, 0.0)
            store_before = extrap_first * (tm_place * hour_dev).astype(jnp.float32)
        else:
            over_lines = (((0,), (0,)), ((), ()))
            wide = lax.dot_general(
                columns_high,
                dual_cat,
                over_lines,
                preferred_element_type=jnp.float32,
            )
            narrow = lax.dot_general(
                columns_low, dual_cat[:, :hour_dev], over_lines, preferred_element_type=jnp.float32
            )
            unit_price = scatter_line(wide[:, :hour_dev] + wide[:, hour_dev:] + narrow, 3)
            ramp_edge, store_after = gathered(
                ramp_dual[:, 0], jnp.sum(store_dual, axis=1), "tm", -1
            )
            ramp_next = jnp.concatenate([ramp_dual[:, 1:], ramp_edge[:, None]], axis=1)
            suffix = exact(store_dual, backward_table) + store_after[:, None]
            gradient = (
                cost[:, None]
                + balance_dual[None, :]
                + unit_price
                + ramp_dual
                - ramp_next
                + storage[:, None] * suffix
            )
            updated = jnp.clip(
                generation - PRIMAL_STEP * gradient, lower_limit[:, None], upper_limit[:, None]
            )
            extrap = 2.0 * updated - generation
            extrap_all = gather_line(extrap, 2).reshape(-1, hour_dev)
            change = extrap_all - first_all.reshape(-1)[:, None]
            line_dual, dual_cat, surplus = flow_step(
                columns_high,
                columns_low,
                jnp.concatenate(parts(change), axis=1),
                rating,
                flow_first,
                line_dual,
                eight(jnp.sum(extrap_all, axis=0) - load_total),
            )
            prev_edge, store_before = gathered(extrap[:, -1], jnp.sum(extrap, axis=1), "tm", 1)
        if iteration == ITERS - 1:
            return (updated, line_dual)
        balance_dual = balance_dual + surplus[0] / UNITS
        previous = jnp.concatenate([prev_edge[:, None], extrap[:, :-1]], axis=1)
        moved = ramp_dual + DUAL_STEP * (extrap - previous) * hour_mask
        ramp_dual = moved - jnp.clip(moved, -DUAL_STEP * ramp[:, None], DUAL_STEP * ramp[:, None])
        running = exact(extrap, forward_table) + store_before[:, None]
        moved = store_dual + DUAL_STEP * storage[:, None] * running
        store_dual = moved - jnp.clip(
            moved, -DUAL_STEP * energy[:, None], DUAL_STEP * energy[:, None]
        )
        generation = updated


def solution(mesh):
    return jax.shard_map(
        on_device,
        mesh=mesh,
        in_specs=(
            P("line", "bus"),
            P("bus", "tm"),
            P(("line", "bus")),
            P(("line", "bus")),
            P(("line", "bus")),
            P(("line", "bus")),
            P("line"),
        ),
        out_specs=(P(("line", "bus"), "tm"), P("line", "tm")),
        check_vma=False,
    )
```

```python
import functools

import jax
import jax.numpy as jnp
from jax import lax
from jax.experimental import pallas as pl
from jax.experimental.pallas import tpu as pltpu
from jax.sharding import PartitionSpec as P

UNITS = 4096
ITERS = 4
MESH = pl.DeviceIdType.MESH


RAMP_RATES = (0.1, 0.2, 0.4, 0.5)
COST_FACTORS = (1.0, 1.5, 3.0, 0.05)
PRIMAL_STEP = 0.5
DUAL_STEP = 0.5


def unit_tables(unit_type, unit_limit, unit_cost):
    capacity = unit_limit.astype(jnp.float32) / 100.0
    kinds = (unit_type[:, None] == jnp.arange(4, dtype=jnp.int32)[None, :]).astype(jnp.float32)
    rates = jnp.sum(kinds * jnp.array(RAMP_RATES, jnp.float32)[None, :], axis=1)
    factors = jnp.sum(kinds * jnp.array(COST_FACTORS, jnp.float32)[None, :], axis=1)
    storage = kinds[:, 3]
    return (
        unit_cost * factors,
        -capacity * storage,
        capacity,
        rates * capacity,
        storage,
        2.0 * capacity,
    )


def parts(value):
    high = lax.reduce_precision(value, 8, 7)
    return high.astype(jnp.bfloat16), (value - high).astype(jnp.bfloat16)


def exact(left, right):
    return jnp.dot(left, right, precision=lax.Precision.HIGHEST, preferred_element_type=jnp.float32)


def stages(steps, tile, part, there, chips, done, sems):
    a_send, a_recv, b_send, b_recv, c_send, c_recv = sems
    bus = lax.axis_index("bus")
    chip_count = chips.shape[0]
    core, chip = lax.rem(bus, 2), lax.div(bus, 2)
    sibling = bus + 1 - 2 * core
    pairs = steps // 2
    half = pairs * tile
    mine, other = core * half, (1 - core) * half
    partners = [lax.rem(chip + j, chip_count) * 2 + core for j in range(1, chip_count)]

    def rows(begin, size):
        return pl.ds(pl.multiple_of(begin, 8), size)

    def copy(source, target, send_sem, recv_sem, peer):
        return pltpu.make_async_remote_copy(
            src_ref=source,
            dst_ref=target,
            send_sem=send_sem,
            recv_sem=recv_sem,
            device_id={"bus": peer},
            device_id_type=MESH,
        )

    def size_of(k):
        return 8 if isinstance(k, int) and k == pairs else tile

    def first(k):
        begin = 2 * half if isinstance(k, int) and k == pairs else other + k * tile
        return copy(
            part.at[rows(begin, size_of(k))],
            there.at[rows(k * tile, size_of(k))],
            a_send.at[k], a_recv.at[k], sibling,
        )

    def cross(k):
        place = chips.at[chip, rows(k * tile, size_of(k))]
        return [
            copy(place, place, b_send.at[j, k], b_recv.at[j, k], peer)
            for j, peer in enumerate(partners)
        ]

    def last(k):
        place = done.at[rows(mine + k * tile, tile)]
        return copy(place, place, c_send.at[k], c_recv.at[k], sibling)

    def enter():
        barrier = pltpu.get_barrier_semaphore()
        for peer in [sibling] + partners:
            pl.semaphore_signal(barrier, inc=1, device_id={"bus": peer}, device_id_type=MESH)
        pl.semaphore_wait(barrier, 1 + len(partners))

    def halve(k):
        first(k).wait_recv()
        begin = 2 * half if isinstance(k, int) and k == pairs else mine + k * tile
        here = rows(k * tile, size_of(k))
        chips[chip, here, :] = part[rows(begin, size_of(k)), :] + there[here, :]
        for each in cross(k):
            each.start()

    def total(k):
        for each in cross(k):
            each.wait_recv()
        here = rows(k * tile, size_of(k))
        value = chips[0, here, :]
        for c in range(1, chip_count):
            value = value + chips[c, here, :]
        return value

    def end():
        for k in range(pairs + 1):
            first(k).wait_send()
            for each in cross(k):
                each.wait_send()
        for k in range(pairs):
            last(k).wait_send()

    return enter, first, halve, total, last, end, rows, mine, other


def run_stages(steps, tile, make_tile, update, extra_ref, extra_out, part, there, chips, done, sems):
    enter, first, halve, total, last, end, rows, mine, other = stages(
        steps, tile, part, there, chips, done, sems
    )
    i = pl.program_id(0)
    pairs = steps // 2
    half = pairs * tile
    k = i // 2

    @pl.when(i == 0)
    def _():
        enter()
        part[2 * half:2 * half + 8, :] = extra_ref[...]
        first(pairs).start()

    part[rows((i % 2) * half + k * tile, tile), :] = make_tile()

    @pl.when(i == 1)
    def _():
        halve(pairs)

    @pl.when(i % 2 == 1)
    def _():
        first(k).start()

        @pl.when(k >= 1)
        def _():
            halve(k - 1)

    @pl.when(i == steps - 1)
    def _():
        halve(pairs - 1)
        for c in range(pairs):
            here = rows(mine + c * tile, tile)
            done[here, :] = total(c)
            last(c).start()
            update(here)
        extra_out[...] = total(pairs)
        for c in range(pairs):
            last(c).wait_recv()
            update(rows(other + c * tile, tile))
        end()


def store_dual_parts(moved, rating, here, dual_out, cat_out):
    hours = moved.shape[1]
    bound = DUAL_STEP * rating
    dual = moved - jnp.clip(moved, -bound, bound)
    high = dual.astype(jnp.bfloat16)
    dual_out[here, :] = dual
    cat_out[here, :hours] = high
    cat_out[here, hours:] = (dual - high.astype(jnp.float32)).astype(jnp.bfloat16)


def setup_kernel(
    groups, units, sub, steps, tile,
    ptdf_ref, pick_ref, load_ref, rating_ref, extra_ref,
    high_ref, low_ref, flow_out, dual_out, cat_out, extra_out,
    part, there, chips, done, *sems,
):
    hours = part.shape[1]

    def make_tile():
        flow = jnp.zeros((tile, hours), jnp.float32)
        for g in range(groups):
            block = ptdf_ref[:, g * sub:(g + 1) * sub]
            high = block.astype(jnp.bfloat16)
            low = (block - high.astype(jnp.float32)).astype(jnp.bfloat16)
            pick = pick_ref[g * sub:(g + 1) * sub, :]
            load = load_ref[g * sub:(g + 1) * sub, :]
            high_ref[g] = jnp.dot(
                high, pick, preferred_element_type=jnp.float32
            ).astype(jnp.bfloat16)
            low_ref[g] = jnp.dot(
                low, pick, preferred_element_type=jnp.float32
            ).astype(jnp.bfloat16)
            wide = jnp.dot(high, load, preferred_element_type=jnp.float32)
            flow += wide[:, :hours] + wide[:, hours:]
            flow += jnp.dot(low, load[:, :hours], preferred_element_type=jnp.float32)
        return flow

    def update(here):
        flow = done[here, :]
        flow_out[here, :] = flow
        store_dual_parts(DUAL_STEP * flow, rating_ref[here, :], here, dual_out, cat_out)

    run_stages(
        steps, tile, make_tile, update, extra_ref, extra_out, part, there, chips, done, sems
    )


def flow_kernel(
    steps, tile,
    high_ref, low_ref, change_ref, rating_ref, flow_ref, dual_ref, extra_ref,
    dual_out, cat_out, extra_out,
    part, there, chips, done, *sems,
):
    hours = part.shape[1]

    def make_tile():
        flow = jnp.zeros((tile, hours), jnp.float32)
        for g in range(high_ref.shape[0]):
            wide = jnp.dot(high_ref[g], change_ref[g], preferred_element_type=jnp.float32)
            flow += wide[:, :hours] + wide[:, hours:]
            flow += jnp.dot(
                low_ref[g], change_ref[g, :, :hours], preferred_element_type=jnp.float32
            )
        return flow

    def update(here):
        moved = dual_ref[here, :] + DUAL_STEP * (flow_ref[here, :] + done[here, :])
        store_dual_parts(moved, rating_ref[here, :], here, dual_out, cat_out)

    run_stages(
        steps, tile, make_tile, update, extra_ref, extra_out, part, there, chips, done, sems
    )


def tiles_of(lines):
    half = lines // 2
    sizes = (384, 320, 240, 192, 160, 128, 96, 64, 48, 32, 16)
    tile = next(t for t in sizes if half % t == 0)
    return 2 * (half // tile), tile


def whole(shape):
    return pl.BlockSpec(shape, lambda i: (0,) * len(shape), pipeline_mode=pl.Buffered(1))


def flow_scratch(lines, hours, steps):
    chip_count, pairs = lax.axis_size("bus") // 2, steps // 2
    first = pltpu.SemaphoreType.DMA((pairs + 1,))
    many = pltpu.SemaphoreType.DMA((chip_count - 1, pairs + 1))
    last = pltpu.SemaphoreType.DMA((pairs,))
    return [
        pltpu.VMEM((lines + 8, hours), jnp.float32),
        pltpu.VMEM((lines // 2 + 8, hours), jnp.float32),
        pltpu.VMEM((chip_count, lines // 2 + 8, hours), jnp.float32),
        pltpu.VMEM((lines, hours), jnp.float32),
        first, first, many, many, last, last,
    ]


def set_up(ptdf, pick, load, rating, extra, groups, units, sub):
    lines, buses = ptdf.shape
    hours = rating.shape[1]
    steps, tile = tiles_of(lines)
    chosen = groups * units
    pairs = steps // 2

    def order(i):
        return ((i % 2) * pairs + i // 2, 0)

    def grouped(i):
        return (0, (i % 2) * pairs + i // 2, 0)

    full = whole((lines, hours))
    return pl.pallas_call(
        functools.partial(setup_kernel, groups, units, sub, steps, tile),
        grid=(steps,),
        in_specs=[
            pl.BlockSpec((tile, buses), order),
            whole((buses, units)),
            whole((buses, 2 * hours)),
            full,
            whole((8, hours)),
        ],
        out_specs=[
            pl.BlockSpec((groups, tile, units), grouped),
            pl.BlockSpec((groups, tile, units), grouped),
            full,
            full,
            whole((lines, 2 * hours)),
            whole((8, hours)),
        ],
        out_shape=[
            jax.ShapeDtypeStruct((groups, lines, units), jnp.bfloat16),
            jax.ShapeDtypeStruct((groups, lines, units), jnp.bfloat16),
            jax.ShapeDtypeStruct((lines, hours), jnp.float32),
            jax.ShapeDtypeStruct((lines, hours), jnp.float32),
            jax.ShapeDtypeStruct((lines, 2 * hours), jnp.bfloat16),
            jax.ShapeDtypeStruct((8, hours), jnp.float32),
        ],
        scratch_shapes=flow_scratch(lines, hours, steps),
        compiler_params=pltpu.CompilerParams(
            collective_id=0, has_side_effects=True, vmem_limit_bytes=52 * 1024 * 1024
        ),
        cost_estimate=pl.CostEstimate(
            flops=4 * lines * buses * (units + 2 * hours),
            bytes_accessed=4 * lines * (buses + chosen + hours),
            transcendentals=0,
        ),
        name="first_flow",
    )(ptdf, pick, load, rating, extra)


def flow_step(high, low, change, rating, flow_first, dual, extra):
    groups, lines, units = high.shape
    chosen = groups * units
    hours = dual.shape[1]
    steps, tile = tiles_of(lines)
    pairs = steps // 2

    def grouped(i):
        return (0, (i % 2) * pairs + i // 2, 0)

    full = whole((lines, hours))
    return pl.pallas_call(
        functools.partial(flow_kernel, steps, tile),
        grid=(steps,),
        in_specs=[
            pl.BlockSpec((groups, tile, units), grouped),
            pl.BlockSpec((groups, tile, units), grouped),
            whole((groups, units, 2 * hours)),
            full,
            full,
            full,
            whole((8, hours)),
        ],
        out_specs=[full, whole((lines, 2 * hours)), whole((8, hours))],
        out_shape=[
            jax.ShapeDtypeStruct((lines, hours), jnp.float32),
            jax.ShapeDtypeStruct((lines, 2 * hours), jnp.bfloat16),
            jax.ShapeDtypeStruct((8, hours), jnp.float32),
        ],
        scratch_shapes=flow_scratch(lines, hours, steps),
        compiler_params=pltpu.CompilerParams(
            collective_id=4, has_side_effects=True, vmem_limit_bytes=44 * 1024 * 1024
        ),
        cost_estimate=pl.CostEstimate(
            flops=6 * lines * chosen * hours,
            bytes_accessed=4 * lines * (chosen + 6 * hours),
            transcendentals=0,
        ),
        name="flow_step",
    )(high, low, change, rating, flow_first, dual, extra)


def greet(axis):
    me, count = lax.axis_index(axis), lax.axis_size(axis)
    peers = [lax.rem(me + j, count) for j in range(1, count)]
    barrier = pltpu.get_barrier_semaphore()
    for peer in peers:
        pl.semaphore_signal(barrier, inc=1, device_id={axis: peer}, device_id_type=MESH)
    pl.semaphore_wait(barrier, count - 1)
    return me, peers


def gather_kernel(block_ref, out_ref, send_sem, recv_sem):
    me, peers = greet("line")
    own = out_ref.at[me]
    copies = [
        pltpu.make_async_remote_copy(
            src_ref=block_ref,
            dst_ref=own,
            send_sem=send_sem.at[j],
            recv_sem=recv_sem.at[j],
            device_id={"line": peer},
            device_id_type=MESH,
        )
        for j, peer in enumerate(peers)
    ]
    for copy in copies:
        copy.start()
    out_ref[me] = block_ref[...]
    for copy in copies:
        copy.wait_recv()
    for copy in copies:
        copy.wait_send()


def unit_kernel(
    high_ref, low_ref, cat_ref, base_ref, info_ref, generation_ref, constant_ref,
    updated_out, extrap_out, change_out, earlier_out, surplus_out,
    high, low, flat, pieces, slots, later, own, everyone, earlier,
    load_sem, price_send, price_recv, later_send, later_recv,
    change_send, change_recv, earlier_send, earlier_recv,
):
    hours = base_ref.shape[1]
    me, count = lax.axis_index("line"), lax.axis_size("line")
    now, spans = lax.axis_index("tm"), lax.axis_size("tm")
    peers = [lax.rem(me + j, count) for j in range(1, count)] + [me]
    sides = [lax.rem(now + j, spans) for j in range(1, spans)]
    loads = []
    for j, peer in enumerate(peers):
        loads.append(pltpu.make_async_copy(high_ref.at[peer], high.at[j], load_sem.at[0, j]))
        loads.append(pltpu.make_async_copy(low_ref.at[peer], low.at[j], load_sem.at[1, j]))
    for load in loads:
        load.start()

    barrier = pltpu.get_barrier_semaphore()
    for peer in peers[:-1]:
        pl.semaphore_signal(barrier, inc=1, device_id={"line": peer}, device_id_type=MESH)
    for side in sides:
        pl.semaphore_signal(barrier, inc=1, device_id={"tm": side}, device_id_type=MESH)
    pl.semaphore_wait(barrier, count - 1 + spans - 1)

    def send(source, target, send_sem, recv_sem, where):
        copy = pltpu.make_async_remote_copy(
            src_ref=source,
            dst_ref=target,
            send_sem=send_sem,
            recv_sem=recv_sem,
            device_id=where,
            device_id_type=MESH,
        )
        copy.start()
        return copy

    own[0] = info_ref[...]
    hour_copies = [
        send(own.at[0], later.at[j], later_send.at[j], later_recv.at[j], {"tm": side})
        for j, side in enumerate(sides)
    ]
    flat[...] = cat_ref[...].T
    price_copies = []
    for j, peer in enumerate(peers):
        loads[2 * j].wait()
        loads[2 * j + 1].wait()
        wide = jnp.dot(flat[...], high[j], preferred_element_type=jnp.float32)
        narrow = jnp.dot(flat[:hours, :], low[j], preferred_element_type=jnp.float32)
        pieces[j] = (wide[:hours] + wide[hours:] + narrow).T
        if j < count - 1:
            price_copies.append(
                send(pieces.at[j], slots.at[j], price_send.at[j], price_recv.at[j], {"line": peer})
            )
    info = info_ref[...]
    gradient = base_ref[...]
    for copy in hour_copies:
        copy.wait_recv()
    lane = lax.broadcasted_iota(jnp.int32, gradient.shape, 1)
    store_after = jnp.zeros_like(info[:, 1:2])
    for j in range(len(sides)):
        source = lax.rem(now - (j + 1) + spans, spans)
        there = later[j]
        after = jnp.where(source > now, 1.0, 0.0)
        beside = jnp.where(source == now + 1, 1.0, 0.0)
        store_after = store_after + after * there[:, 1:2]
        gradient = gradient - jnp.where(lane == hours - 1, beside * there[:, 0:1], 0.0)
    gradient = gradient + info[:, 2:3] * store_after + pieces[count - 1]
    for j, copy in enumerate(price_copies):
        copy.wait_recv()
        gradient = gradient + slots[j]
    generation = generation_ref[...]
    updated = jnp.clip(generation - PRIMAL_STEP * gradient, info[:, 3:4], info[:, 4:5])
    extrap = 2.0 * updated - generation
    own[1] = extrap
    everyone[me] = extrap - info[:, 5:6]
    place = everyone.at[me]
    change_copies = [
        send(place, place, change_send.at[j], change_recv.at[j], {"line": peer})
        for j, peer in enumerate(peers[:-1])
    ]
    extrap_copies = [
        send(own.at[1], earlier.at[j], earlier_send.at[j], earlier_recv.at[j], {"tm": side})
        for j, side in enumerate(sides)
    ]
    updated_out[...] = updated
    extrap_out[...] = extrap
    for j, copy in enumerate(extrap_copies):
        copy.wait_recv()
        earlier_out[j] = earlier[j]
    for copy in change_copies:
        copy.wait_recv()
    surplus = constant_ref[...]
    for g in range(count):
        change = everyone[g]
        part = change.astype(jnp.bfloat16)
        change_out[g, :, :hours] = part
        change_out[g, :, hours:] = (change - part.astype(jnp.float32)).astype(jnp.bfloat16)
        surplus = surplus + jnp.sum(change, axis=0, keepdims=True)
    surplus_out[...] = surplus
    for copy in hour_copies + price_copies + change_copies + extrap_copies:
        copy.wait_send()


def unit_step(high, low, cat, base, info, generation, constant):
    groups, lines, units = high.shape
    hours = base.shape[1]
    sides = lax.axis_size("tm") - 1
    block = (units, hours)
    line_sem = pltpu.SemaphoreType.DMA((groups - 1,))
    tm_sem = pltpu.SemaphoreType.DMA((sides,))
    near = pl.BlockSpec(memory_space=pltpu.VMEM)
    far = pl.BlockSpec(memory_space=pl.ANY)
    return pl.pallas_call(
        unit_kernel,
        in_specs=[far, far] + [near] * 5,
        out_specs=[near] * 5,
        out_shape=[
            jax.ShapeDtypeStruct(block, jnp.float32),
            jax.ShapeDtypeStruct(block, jnp.float32),
            jax.ShapeDtypeStruct((groups, units, 2 * hours), jnp.bfloat16),
            jax.ShapeDtypeStruct((sides,) + block, jnp.float32),
            jax.ShapeDtypeStruct((8, hours), jnp.float32),
        ],
        scratch_shapes=[
            pltpu.VMEM((groups, lines, units), jnp.bfloat16),
            pltpu.VMEM((groups, lines, units), jnp.bfloat16),
            pltpu.VMEM((2 * hours, lines), jnp.bfloat16),
            pltpu.VMEM((groups,) + block, jnp.float32),
            pltpu.VMEM((groups - 1,) + block, jnp.float32),
            pltpu.VMEM((sides,) + block, jnp.float32),
            pltpu.VMEM((2,) + block, jnp.float32),
            pltpu.VMEM((groups,) + block, jnp.float32),
            pltpu.VMEM((sides,) + block, jnp.float32),
            pltpu.SemaphoreType.DMA((2, groups)),
            line_sem, line_sem, tm_sem, tm_sem, line_sem, line_sem, tm_sem, tm_sem,
        ],
        compiler_params=pltpu.CompilerParams(
            collective_id=3, has_side_effects=True, vmem_limit_bytes=44 * 1024 * 1024
        ),
        cost_estimate=pl.CostEstimate(
            flops=6 * groups * lines * units * hours,
            bytes_accessed=4 * groups * lines * units,
            transcendentals=0,
        ),
        name="unit_step",
    )(high, low, cat, base, info, generation, constant)


def line_call(kernel, value, shape, slots, ident, name):
    sems = pltpu.SemaphoreType.DMA((lax.axis_size("line") - 1,))
    return pl.pallas_call(
        kernel,
        out_shape=jax.ShapeDtypeStruct(shape, value.dtype),
        in_specs=[pl.BlockSpec(memory_space=pltpu.VMEM)],
        out_specs=pl.BlockSpec(memory_space=pltpu.VMEM),
        scratch_shapes=slots + [sems, sems],
        compiler_params=pltpu.CompilerParams(
            collective_id=ident, has_side_effects=True, vmem_limit_bytes=32 * 1024 * 1024
        ),
        name=name,
    )(value)


def gather_line(value, ident):
    shape = (lax.axis_size("line"),) + value.shape
    return line_call(gather_kernel, value, shape, [], ident, "gather_line")


def on_device(ptdf_matrix, bus_load, unit_bus, unit_type, unit_limit, unit_cost, line_rating):
    line_place = lax.axis_index("line")
    bus_place = lax.axis_index("bus")
    tm_place = lax.axis_index("tm")
    groups = lax.axis_size("line")
    lines, block_rows = ptdf_matrix.shape
    sub = block_rows // groups
    hour_dev = bus_load.shape[1]
    units = unit_bus.shape[0]
    cost, lower_limit, upper_limit, ramp, storage, energy = unit_tables(
        unit_type, unit_limit, unit_cost
    )
    first = jnp.clip(-PRIMAL_STEP * cost, lower_limit, upper_limit)
    extrap_first = 2.0 * first
    place = (unit_bus - bus_place * block_rows - line_place * sub).astype(jnp.float32)
    both = gather_line(jnp.stack([place, extrap_first] * 4), 1)
    places = both[:, 0].astype(jnp.int32)
    first_all = both[:, 1]
    pick = places[:, None, :] == jnp.arange(sub, dtype=jnp.int32)[None, :, None]
    placed = jnp.sum(jnp.where(pick, first_all[:, None, :], 0.0), axis=2).reshape(block_rows)
    pick = pick.astype(jnp.bfloat16).reshape(block_rows, units)
    injected = placed[:, None] - bus_load
    rating = jnp.broadcast_to(
        (line_rating.astype(jnp.float32) / 100.0)[:, None], (lines, hour_dev)
    )
    load_total = jnp.sum(bus_load, axis=0)

    def eight(surplus):
        return jnp.broadcast_to(surplus[None, :], (8, hour_dev))

    constant = eight(jnp.sum(first_all) - load_total)
    columns_high, columns_low, flow_first, line_dual, dual_cat, surplus = set_up(
        ptdf_matrix,
        pick,
        jnp.concatenate(parts(injected), axis=1),
        rating,
        constant,
        groups,
        units,
        sub,
    )
    earlier_index = jnp.arange(hour_dev, dtype=jnp.int32)[:, None]
    later_index = jnp.arange(hour_dev, dtype=jnp.int32)[None, :]
    forward_table = (earlier_index <= later_index).astype(jnp.float32)
    backward_table = (earlier_index >= later_index).astype(jnp.float32)
    hour_mask = (tm_place * hour_dev + jnp.arange(hour_dev, dtype=jnp.int32) >= 1).astype(
        jnp.float32
    )[None, :]
    generation = jnp.zeros((units, hour_dev), jnp.float32)
    ramp_dual = jnp.zeros((units, hour_dev), jnp.float32)
    store_dual = jnp.zeros((units, hour_dev), jnp.float32)
    balance_dual = jnp.zeros((hour_dev,), jnp.float32)
    for iteration in range(ITERS):
        if iteration == 0:
            updated = jnp.broadcast_to(first[:, None], (units, hour_dev))
            extrap = 2.0 * updated
            prev_edge = jnp.where(tm_place > 0, extrap_first, 0.0)
            store_before = extrap_first * (tm_place * hour_dev).astype(jnp.float32)
        else:
            ramp_next = jnp.pad(ramp_dual[:, 1:], ((0, 0), (0, 1)))
            suffix = exact(store_dual, backward_table)
            base = (
                cost[:, None]
                + balance_dual[None, :]
                + ramp_dual
                - ramp_next
                + storage[:, None] * suffix
            )
            head = [ramp_dual[:, 0], jnp.sum(store_dual, axis=1), storage]
            tail = [lower_limit, upper_limit, extrap_first]
            info = jnp.pad(jnp.stack(head + tail, axis=1), ((0, 0), (0, hour_dev - 6)))
            updated, extrap, change, there, extra = unit_step(
                columns_high, columns_low, dual_cat, base, info, generation, constant
            )
            line_dual, dual_cat, surplus = flow_step(
                columns_high, columns_low, change, rating, flow_first, line_dual, extra
            )
            prev_edge, store_before = jnp.zeros_like(cost), jnp.zeros_like(cost)
            for j in range(there.shape[0]):
                span_count = lax.axis_size("tm")
                source = (tm_place - (j + 1) + span_count) % span_count
                prev_edge += jnp.where(source == tm_place - 1, there[j, :, -1], 0.0)
                store_before += jnp.where(source < tm_place, jnp.sum(there[j], axis=1), 0.0)
        if iteration == ITERS - 1:
            return (updated, line_dual)
        balance_dual = balance_dual + surplus[0] / UNITS
        previous = jnp.concatenate([prev_edge[:, None], extrap[:, :-1]], axis=1)
        moved = ramp_dual + DUAL_STEP * (extrap - previous) * hour_mask
        ramp_dual = moved - jnp.clip(moved, -DUAL_STEP * ramp[:, None], DUAL_STEP * ramp[:, None])
        running = exact(extrap, forward_table) + store_before[:, None]
        moved = store_dual + DUAL_STEP * storage[:, None] * running
        store_dual = moved - jnp.clip(
            moved, -DUAL_STEP * energy[:, None], DUAL_STEP * energy[:, None]
        )
        generation = updated


def solution(mesh):
    return jax.shard_map(
        on_device,
        mesh=mesh,
        in_specs=(
            P("line", "bus"),
            P("bus", "tm"),
            P(("line", "bus")),
            P(("line", "bus")),
            P(("line", "bus")),
            P(("line", "bus")),
            P("line"),
        ),
        out_specs=(P(("line", "bus"), "tm"), P("line", "tm")),
        check_vma=False,
    )
```

```python
import functools

import jax
import jax.numpy as jnp
from jax import lax
from jax.experimental import pallas as pl
from jax.experimental.pallas import tpu as pltpu
from jax.sharding import PartitionSpec as P

UNITS = 4096
ITERS = 4
MESH = pl.DeviceIdType.MESH


RAMP_RATES = (0.1, 0.2, 0.4, 0.5)
COST_FACTORS = (1.0, 1.5, 3.0, 0.05)
PRIMAL_STEP = 0.5
DUAL_STEP = 0.5


def unit_tables(unit_type, unit_limit, unit_cost):
    capacity = unit_limit.astype(jnp.float32) / 100.0
    kinds = (unit_type[:, None] == jnp.arange(4, dtype=jnp.int32)[None, :]).astype(jnp.float32)
    rates = jnp.sum(kinds * jnp.array(RAMP_RATES, jnp.float32)[None, :], axis=1)
    factors = jnp.sum(kinds * jnp.array(COST_FACTORS, jnp.float32)[None, :], axis=1)
    storage = kinds[:, 3]
    return (
        unit_cost * factors,
        -capacity * storage,
        capacity,
        rates * capacity,
        storage,
        2.0 * capacity,
    )


def parts(value):
    high = lax.reduce_precision(value, 8, 7)
    return high.astype(jnp.bfloat16), (value - high).astype(jnp.bfloat16)


def exact(left, right):
    return jnp.dot(left, right, precision=lax.Precision.HIGHEST, preferred_element_type=jnp.float32)


def stages(steps, tile, part, there, chips, done, sems):
    a_send, a_recv, b_send, b_recv, c_send, c_recv = sems
    bus = lax.axis_index("bus")
    chip_count = chips.shape[0]
    core, chip = lax.rem(bus, 2), lax.div(bus, 2)
    sibling = bus + 1 - 2 * core
    pairs = steps // 2
    half = pairs * tile
    mine, other = core * half, (1 - core) * half
    partners = [lax.rem(chip + j, chip_count) * 2 + core for j in range(1, chip_count)]

    def rows(begin, size):
        return pl.ds(pl.multiple_of(begin, 8), size)

    def copy(source, target, send_sem, recv_sem, peer):
        return pltpu.make_async_remote_copy(
            src_ref=source,
            dst_ref=target,
            send_sem=send_sem,
            recv_sem=recv_sem,
            device_id={"bus": peer},
            device_id_type=MESH,
        )

    def size_of(k):
        return 8 if isinstance(k, int) and k == pairs else tile

    def first(k):
        begin = 2 * half if isinstance(k, int) and k == pairs else other + k * tile
        return copy(
            part.at[rows(begin, size_of(k))],
            there.at[rows(k * tile, size_of(k))],
            a_send.at[k], a_recv.at[k], sibling,
        )

    def cross(k):
        place = chips.at[chip, rows(k * tile, size_of(k))]
        return [
            copy(place, place, b_send.at[j, k], b_recv.at[j, k], peer)
            for j, peer in enumerate(partners)
        ]

    def last(k):
        place = done.at[rows(mine + k * tile, tile)]
        return copy(place, place, c_send.at[k], c_recv.at[k], sibling)

    def enter():
        barrier = pltpu.get_barrier_semaphore()
        for peer in [sibling] + partners:
            pl.semaphore_signal(barrier, inc=1, device_id={"bus": peer}, device_id_type=MESH)
        pl.semaphore_wait(barrier, 1 + len(partners))

    def halve(k):
        first(k).wait_recv()
        begin = 2 * half if isinstance(k, int) and k == pairs else mine + k * tile
        here = rows(k * tile, size_of(k))
        chips[chip, here, :] = part[rows(begin, size_of(k)), :] + there[here, :]
        for each in cross(k):
            each.start()

    def total(k):
        for each in cross(k):
            each.wait_recv()
        here = rows(k * tile, size_of(k))
        value = chips[0, here, :]
        for c in range(1, chip_count):
            value = value + chips[c, here, :]
        return value

    def end():
        for k in range(pairs + 1):
            first(k).wait_send()
            for each in cross(k):
                each.wait_send()
        for k in range(pairs):
            last(k).wait_send()

    return enter, first, halve, total, last, end, rows, mine, other


def run_stages(steps, tile, make_tile, update, extra_ref, extra_out, part, there, chips, done, sems):
    enter, first, halve, total, last, end, rows, mine, other = stages(
        steps, tile, part, there, chips, done, sems
    )
    i = pl.program_id(0)
    pairs = steps // 2
    half = pairs * tile
    k = i // 2

    @pl.when(i == 0)
    def _():
        enter()
        part[2 * half:2 * half + 8, :] = extra_ref[...]
        first(pairs).start()

    part[rows((i % 2) * half + k * tile, tile), :] = make_tile()

    @pl.when(i == 1)
    def _():
        halve(pairs)

    @pl.when(i % 2 == 1)
    def _():
        first(k).start()

        @pl.when(k >= 1)
        def _():
            halve(k - 1)

    @pl.when(i == steps - 1)
    def _():
        halve(pairs - 1)
        for c in range(pairs):
            here = rows(mine + c * tile, tile)
            done[here, :] = total(c)
            last(c).start()
            update(here)
        extra_out[...] = total(pairs)
        for c in range(pairs):
            last(c).wait_recv()
            update(rows(other + c * tile, tile))
        end()


def bring(steps, sems, pairs):
    i = pl.program_id(0)
    copies = [
        pltpu.make_async_copy(source, target, sems.at[j])
        for j, (source, target) in enumerate(pairs)
    ]

    @pl.when(i == 0)
    def _():
        for copy in copies:
            copy.start()

    @pl.when(i == steps - 1)
    def _():
        for copy in copies:
            copy.wait()


def store_dual_parts(moved, rating, here, dual_out, cat_out):
    hours = moved.shape[1]
    bound = DUAL_STEP * rating
    dual = moved - jnp.clip(moved, -bound, bound)
    high = dual.astype(jnp.bfloat16)
    dual_out[here, :] = dual
    cat_out[here, :hours] = high
    cat_out[here, hours:] = (dual - high.astype(jnp.float32)).astype(jnp.bfloat16)


def setup_kernel(
    groups, units, sub, steps, tile,
    ptdf_ref, pick_ref, load_ref, rating_far, extra_ref,
    high_ref, low_ref, flow_out, dual_out, cat_out, extra_out,
    rating_ref, load_sem, part, there, chips, done, *sems,
):
    hours = part.shape[1]
    bring(steps, load_sem, [(rating_far, rating_ref)])

    def make_tile():
        flow = jnp.zeros((tile, hours), jnp.float32)
        for g in range(groups):
            block = ptdf_ref[:, g * sub:(g + 1) * sub]
            high = block.astype(jnp.bfloat16)
            low = (block - high.astype(jnp.float32)).astype(jnp.bfloat16)
            pick = pick_ref[g * sub:(g + 1) * sub, :]
            load = load_ref[g * sub:(g + 1) * sub, :]
            high_ref[g] = jnp.dot(
                high, pick, preferred_element_type=jnp.float32
            ).astype(jnp.bfloat16)
            low_ref[g] = jnp.dot(
                low, pick, preferred_element_type=jnp.float32
            ).astype(jnp.bfloat16)
            wide = jnp.dot(high, load, preferred_element_type=jnp.float32)
            flow += wide[:, :hours] + wide[:, hours:]
            flow += jnp.dot(low, load[:, :hours], preferred_element_type=jnp.float32)
        return flow

    def update(here):
        flow = done[here, :]
        flow_out[here, :] = flow
        store_dual_parts(DUAL_STEP * flow, rating_ref[here, :], here, dual_out, cat_out)

    run_stages(
        steps, tile, make_tile, update, extra_ref, extra_out, part, there, chips, done, sems
    )


def flow_kernel(
    steps, tile,
    high_ref, low_ref, change_ref, rating_far, flow_far, dual_far, extra_ref,
    dual_out, cat_out, extra_out,
    rating_ref, flow_ref, dual_ref, load_sem, part, there, chips, done, *sems,
):
    hours = part.shape[1]
    bring(
        steps, load_sem, [(rating_far, rating_ref), (flow_far, flow_ref), (dual_far, dual_ref)]
    )

    def make_tile():
        flow = jnp.zeros((tile, hours), jnp.float32)
        for g in range(high_ref.shape[0]):
            wide = jnp.dot(high_ref[g], change_ref[g], preferred_element_type=jnp.float32)
            flow += wide[:, :hours] + wide[:, hours:]
            flow += jnp.dot(
                low_ref[g], change_ref[g, :, :hours], preferred_element_type=jnp.float32
            )
        return flow

    def update(here):
        moved = dual_ref[here, :] + DUAL_STEP * (flow_ref[here, :] + done[here, :])
        store_dual_parts(moved, rating_ref[here, :], here, dual_out, cat_out)

    run_stages(
        steps, tile, make_tile, update, extra_ref, extra_out, part, there, chips, done, sems
    )


def tiles_of(lines):
    half = lines // 2
    sizes = (240, 192, 160, 128, 96, 64, 48, 32, 16)
    tile = next(t for t in sizes if half % t == 0)
    return 2 * (half // tile), tile


def whole(shape):
    return pl.BlockSpec(shape, lambda i: (0,) * len(shape), pipeline_mode=pl.Buffered(1))


def flow_scratch(lines, hours, steps):
    chip_count, pairs = lax.axis_size("bus") // 2, steps // 2
    first = pltpu.SemaphoreType.DMA((pairs + 1,))
    many = pltpu.SemaphoreType.DMA((chip_count - 1, pairs + 1))
    last = pltpu.SemaphoreType.DMA((pairs,))
    return [
        pltpu.VMEM((lines + 8, hours), jnp.float32),
        pltpu.VMEM((lines // 2 + 8, hours), jnp.float32),
        pltpu.VMEM((chip_count, lines // 2 + 8, hours), jnp.float32),
        pltpu.VMEM((lines, hours), jnp.float32),
        first, first, many, many, last, last,
    ]


def set_up(ptdf, pick, load, rating, extra, groups, units, sub):
    lines, buses = ptdf.shape
    hours = rating.shape[1]
    steps, tile = tiles_of(lines)
    chosen = groups * units
    pairs = steps // 2

    def order(i):
        return ((i % 2) * pairs + i // 2, 0)

    def grouped(i):
        return (0, (i % 2) * pairs + i // 2, 0)

    full, far = whole((lines, hours)), pl.BlockSpec(memory_space=pl.ANY)
    kept = pltpu.VMEM((lines, hours), jnp.float32)
    return pl.pallas_call(
        functools.partial(setup_kernel, groups, units, sub, steps, tile),
        grid=(steps,),
        in_specs=[
            pl.BlockSpec((tile, buses), order),
            whole((buses, units)),
            whole((buses, 2 * hours)),
            far,
            whole((8, hours)),
        ],
        out_specs=[
            pl.BlockSpec((groups, tile, units), grouped),
            pl.BlockSpec((groups, tile, units), grouped),
            full,
            full,
            whole((lines, 2 * hours)),
            whole((8, hours)),
        ],
        out_shape=[
            jax.ShapeDtypeStruct((groups, lines, units), jnp.bfloat16),
            jax.ShapeDtypeStruct((groups, lines, units), jnp.bfloat16),
            jax.ShapeDtypeStruct((lines, hours), jnp.float32),
            jax.ShapeDtypeStruct((lines, hours), jnp.float32),
            jax.ShapeDtypeStruct((lines, 2 * hours), jnp.bfloat16),
            jax.ShapeDtypeStruct((8, hours), jnp.float32),
        ],
        scratch_shapes=[kept, pltpu.SemaphoreType.DMA((1,))] + flow_scratch(lines, hours, steps),
        compiler_params=pltpu.CompilerParams(
            collective_id=0, has_side_effects=True, vmem_limit_bytes=52 * 1024 * 1024
        ),
        cost_estimate=pl.CostEstimate(
            flops=4 * lines * buses * (units + 2 * hours),
            bytes_accessed=4 * lines * (buses + chosen + hours),
            transcendentals=0,
        ),
        name="first_flow",
    )(ptdf, pick, load, rating, extra)


def flow_step(high, low, change, rating, flow_first, dual, extra):
    groups, lines, units = high.shape
    chosen = groups * units
    hours = dual.shape[1]
    steps, tile = tiles_of(lines)
    pairs = steps // 2

    def grouped(i):
        return (0, (i % 2) * pairs + i // 2, 0)

    full, far = whole((lines, hours)), pl.BlockSpec(memory_space=pl.ANY)
    kept = pltpu.VMEM((lines, hours), jnp.float32)
    return pl.pallas_call(
        functools.partial(flow_kernel, steps, tile),
        grid=(steps,),
        in_specs=[
            pl.BlockSpec((groups, tile, units), grouped),
            pl.BlockSpec((groups, tile, units), grouped),
            whole((groups, units, 2 * hours)),
            far,
            far,
            far,
            whole((8, hours)),
        ],
        out_specs=[full, whole((lines, 2 * hours)), whole((8, hours))],
        out_shape=[
            jax.ShapeDtypeStruct((lines, hours), jnp.float32),
            jax.ShapeDtypeStruct((lines, 2 * hours), jnp.bfloat16),
            jax.ShapeDtypeStruct((8, hours), jnp.float32),
        ],
        scratch_shapes=[kept] * 3 + [pltpu.SemaphoreType.DMA((3,))]
        + flow_scratch(lines, hours, steps),
        compiler_params=pltpu.CompilerParams(
            collective_id=4, has_side_effects=True, vmem_limit_bytes=44 * 1024 * 1024
        ),
        cost_estimate=pl.CostEstimate(
            flops=6 * lines * chosen * hours,
            bytes_accessed=4 * lines * (chosen + 6 * hours),
            transcendentals=0,
        ),
        name="flow_step",
    )(high, low, change, rating, flow_first, dual, extra)


def greet(axis):
    me, count = lax.axis_index(axis), lax.axis_size(axis)
    peers = [lax.rem(me + j, count) for j in range(1, count)]
    barrier = pltpu.get_barrier_semaphore()
    for peer in peers:
        pl.semaphore_signal(barrier, inc=1, device_id={axis: peer}, device_id_type=MESH)
    pl.semaphore_wait(barrier, count - 1)
    return me, peers


def gather_kernel(block_ref, out_ref, send_sem, recv_sem):
    me, peers = greet("line")
    own = out_ref.at[me]
    copies = [
        pltpu.make_async_remote_copy(
            src_ref=block_ref,
            dst_ref=own,
            send_sem=send_sem.at[j],
            recv_sem=recv_sem.at[j],
            device_id={"line": peer},
            device_id_type=MESH,
        )
        for j, peer in enumerate(peers)
    ]
    for copy in copies:
        copy.start()
    out_ref[me] = block_ref[...]
    for copy in copies:
        copy.wait_recv()
    for copy in copies:
        copy.wait_send()


def unit_kernel(
    high_ref, low_ref, cat_ref, base_ref, info_ref, generation_ref, constant_ref,
    updated_out, extrap_out, change_out, earlier_out, surplus_out,
    high, low, flat, pieces, slots, later, own, everyone, earlier,
    load_sem, price_send, price_recv, later_send, later_recv,
    change_send, change_recv, earlier_send, earlier_recv,
):
    hours = base_ref.shape[1]
    me, count = lax.axis_index("line"), lax.axis_size("line")
    now, spans = lax.axis_index("tm"), lax.axis_size("tm")
    peers = [lax.rem(me + j, count) for j in range(1, count)] + [me]
    sides = [lax.rem(now + j, spans) for j in range(1, spans)]
    loads = []
    for j, peer in enumerate(peers):
        loads.append(pltpu.make_async_copy(high_ref.at[peer], high.at[j], load_sem.at[0, j]))
        loads.append(pltpu.make_async_copy(low_ref.at[peer], low.at[j], load_sem.at[1, j]))
    for load in loads:
        load.start()

    barrier = pltpu.get_barrier_semaphore()
    for peer in peers[:-1]:
        pl.semaphore_signal(barrier, inc=1, device_id={"line": peer}, device_id_type=MESH)
    for side in sides:
        pl.semaphore_signal(barrier, inc=1, device_id={"tm": side}, device_id_type=MESH)
    pl.semaphore_wait(barrier, count - 1 + spans - 1)

    def send(source, target, send_sem, recv_sem, where):
        copy = pltpu.make_async_remote_copy(
            src_ref=source,
            dst_ref=target,
            send_sem=send_sem,
            recv_sem=recv_sem,
            device_id=where,
            device_id_type=MESH,
        )
        copy.start()
        return copy

    own[0] = info_ref[...]
    hour_copies = [
        send(own.at[0], later.at[j], later_send.at[j], later_recv.at[j], {"tm": side})
        for j, side in enumerate(sides)
    ]
    flat[...] = cat_ref[...].T
    price_copies = []
    for j, peer in enumerate(peers):
        loads[2 * j].wait()
        loads[2 * j + 1].wait()
        wide = jnp.dot(flat[...], high[j], preferred_element_type=jnp.float32)
        narrow = jnp.dot(flat[:hours, :], low[j], preferred_element_type=jnp.float32)
        pieces[j] = (wide[:hours] + wide[hours:] + narrow).T
        if j < count - 1:
            price_copies.append(
                send(pieces.at[j], slots.at[j], price_send.at[j], price_recv.at[j], {"line": peer})
            )
    info = info_ref[...]
    gradient = base_ref[...]
    for copy in hour_copies:
        copy.wait_recv()
    lane = lax.broadcasted_iota(jnp.int32, gradient.shape, 1)
    store_after = jnp.zeros_like(info[:, 1:2])
    for j in range(len(sides)):
        source = lax.rem(now - (j + 1) + spans, spans)
        there = later[j]
        after = jnp.where(source > now, 1.0, 0.0)
        beside = jnp.where(source == now + 1, 1.0, 0.0)
        store_after = store_after + after * there[:, 1:2]
        gradient = gradient - jnp.where(lane == hours - 1, beside * there[:, 0:1], 0.0)
    gradient = gradient + info[:, 2:3] * store_after + pieces[count - 1]
    for j, copy in enumerate(price_copies):
        copy.wait_recv()
        gradient = gradient + slots[j]
    generation = generation_ref[...]
    updated = jnp.clip(generation - PRIMAL_STEP * gradient, info[:, 3:4], info[:, 4:5])
    extrap = 2.0 * updated - generation
    own[1] = extrap
    everyone[me] = extrap - info[:, 5:6]
    place = everyone.at[me]
    change_copies = [
        send(place, place, change_send.at[j], change_recv.at[j], {"line": peer})
        for j, peer in enumerate(peers[:-1])
    ]
    extrap_copies = [
        send(own.at[1], earlier.at[j], earlier_send.at[j], earlier_recv.at[j], {"tm": side})
        for j, side in enumerate(sides)
    ]
    updated_out[...] = updated
    extrap_out[...] = extrap
    for j, copy in enumerate(extrap_copies):
        copy.wait_recv()
        earlier_out[j] = earlier[j]
    for copy in change_copies:
        copy.wait_recv()
    surplus = constant_ref[...]
    for g in range(count):
        change = everyone[g]
        part = change.astype(jnp.bfloat16)
        change_out[g, :, :hours] = part
        change_out[g, :, hours:] = (change - part.astype(jnp.float32)).astype(jnp.bfloat16)
        surplus = surplus + jnp.sum(change, axis=0, keepdims=True)
    surplus_out[...] = surplus
    for copy in hour_copies + price_copies + change_copies + extrap_copies:
        copy.wait_send()


def unit_step(high, low, cat, base, info, generation, constant):
    groups, lines, units = high.shape
    hours = base.shape[1]
    sides = lax.axis_size("tm") - 1
    block = (units, hours)
    line_sem = pltpu.SemaphoreType.DMA((groups - 1,))
    tm_sem = pltpu.SemaphoreType.DMA((sides,))
    near = pl.BlockSpec(memory_space=pltpu.VMEM)
    far = pl.BlockSpec(memory_space=pl.ANY)
    return pl.pallas_call(
        unit_kernel,
        in_specs=[far, far] + [near] * 5,
        out_specs=[near] * 5,
        out_shape=[
            jax.ShapeDtypeStruct(block, jnp.float32),
            jax.ShapeDtypeStruct(block, jnp.float32),
            jax.ShapeDtypeStruct((groups, units, 2 * hours), jnp.bfloat16),
            jax.ShapeDtypeStruct((sides,) + block, jnp.float32),
            jax.ShapeDtypeStruct((8, hours), jnp.float32),
        ],
        scratch_shapes=[
            pltpu.VMEM((groups, lines, units), jnp.bfloat16),
            pltpu.VMEM((groups, lines, units), jnp.bfloat16),
            pltpu.VMEM((2 * hours, lines), jnp.bfloat16),
            pltpu.VMEM((groups,) + block, jnp.float32),
            pltpu.VMEM((groups - 1,) + block, jnp.float32),
            pltpu.VMEM((sides,) + block, jnp.float32),
            pltpu.VMEM((2,) + block, jnp.float32),
            pltpu.VMEM((groups,) + block, jnp.float32),
            pltpu.VMEM((sides,) + block, jnp.float32),
            pltpu.SemaphoreType.DMA((2, groups)),
            line_sem, line_sem, tm_sem, tm_sem, line_sem, line_sem, tm_sem, tm_sem,
        ],
        compiler_params=pltpu.CompilerParams(
            collective_id=3, has_side_effects=True, vmem_limit_bytes=44 * 1024 * 1024
        ),
        cost_estimate=pl.CostEstimate(
            flops=6 * groups * lines * units * hours,
            bytes_accessed=4 * groups * lines * units,
            transcendentals=0,
        ),
        name="unit_step",
    )(high, low, cat, base, info, generation, constant)


def line_call(kernel, value, shape, slots, ident, name):
    sems = pltpu.SemaphoreType.DMA((lax.axis_size("line") - 1,))
    return pl.pallas_call(
        kernel,
        out_shape=jax.ShapeDtypeStruct(shape, value.dtype),
        in_specs=[pl.BlockSpec(memory_space=pltpu.VMEM)],
        out_specs=pl.BlockSpec(memory_space=pltpu.VMEM),
        scratch_shapes=slots + [sems, sems],
        compiler_params=pltpu.CompilerParams(
            collective_id=ident, has_side_effects=True, vmem_limit_bytes=32 * 1024 * 1024
        ),
        name=name,
    )(value)


def gather_line(value, ident):
    shape = (lax.axis_size("line"),) + value.shape
    return line_call(gather_kernel, value, shape, [], ident, "gather_line")


def on_device(ptdf_matrix, bus_load, unit_bus, unit_type, unit_limit, unit_cost, line_rating):
    line_place = lax.axis_index("line")
    bus_place = lax.axis_index("bus")
    tm_place = lax.axis_index("tm")
    groups = lax.axis_size("line")
    lines, block_rows = ptdf_matrix.shape
    sub = block_rows // groups
    hour_dev = bus_load.shape[1]
    units = unit_bus.shape[0]
    cost, lower_limit, upper_limit, ramp, storage, energy = unit_tables(
        unit_type, unit_limit, unit_cost
    )
    first = jnp.clip(-PRIMAL_STEP * cost, lower_limit, upper_limit)
    extrap_first = 2.0 * first
    place = (unit_bus - bus_place * block_rows - line_place * sub).astype(jnp.float32)
    both = gather_line(jnp.stack([place, extrap_first] * 4), 1)
    places = both[:, 0].astype(jnp.int32)
    first_all = both[:, 1]
    pick = places[:, None, :] == jnp.arange(sub, dtype=jnp.int32)[None, :, None]
    placed = jnp.sum(jnp.where(pick, first_all[:, None, :], 0.0), axis=2).reshape(block_rows)
    pick = pick.astype(jnp.bfloat16).reshape(block_rows, units)
    injected = placed[:, None] - bus_load
    rating = jnp.broadcast_to(
        (line_rating.astype(jnp.float32) / 100.0)[:, None], (lines, hour_dev)
    )
    load_total = jnp.sum(bus_load, axis=0)

    def eight(surplus):
        return jnp.broadcast_to(surplus[None, :], (8, hour_dev))

    constant = eight(jnp.sum(first_all) - load_total)
    columns_high, columns_low, flow_first, line_dual, dual_cat, surplus = set_up(
        ptdf_matrix,
        pick,
        jnp.concatenate(parts(injected), axis=1),
        rating,
        constant,
        groups,
        units,
        sub,
    )
    earlier_index = jnp.arange(hour_dev, dtype=jnp.int32)[:, None]
    later_index = jnp.arange(hour_dev, dtype=jnp.int32)[None, :]
    forward_table = (earlier_index <= later_index).astype(jnp.float32)
    backward_table = (earlier_index >= later_index).astype(jnp.float32)
    hour_mask = (tm_place * hour_dev + jnp.arange(hour_dev, dtype=jnp.int32) >= 1).astype(
        jnp.float32
    )[None, :]
    generation = jnp.zeros((units, hour_dev), jnp.float32)
    ramp_dual = jnp.zeros((units, hour_dev), jnp.float32)
    store_dual = jnp.zeros((units, hour_dev), jnp.float32)
    balance_dual = jnp.zeros((hour_dev,), jnp.float32)
    for iteration in range(ITERS):
        if iteration == 0:
            updated = jnp.broadcast_to(first[:, None], (units, hour_dev))
            extrap = 2.0 * updated
            prev_edge = jnp.where(tm_place > 0, extrap_first, 0.0)
            store_before = extrap_first * (tm_place * hour_dev).astype(jnp.float32)
        else:
            ramp_next = jnp.pad(ramp_dual[:, 1:], ((0, 0), (0, 1)))
            suffix = exact(store_dual, backward_table)
            base = (
                cost[:, None]
                + balance_dual[None, :]
                + ramp_dual
                - ramp_next
                + storage[:, None] * suffix
            )
            head = [ramp_dual[:, 0], jnp.sum(store_dual, axis=1), storage]
            tail = [lower_limit, upper_limit, extrap_first]
            info = jnp.pad(jnp.stack(head + tail, axis=1), ((0, 0), (0, hour_dev - 6)))
            updated, extrap, change, there, extra = unit_step(
                columns_high, columns_low, dual_cat, base, info, generation, constant
            )
            line_dual, dual_cat, surplus = flow_step(
                columns_high, columns_low, change, rating, flow_first, line_dual, extra
            )
            prev_edge, store_before = jnp.zeros_like(cost), jnp.zeros_like(cost)
            for j in range(there.shape[0]):
                span_count = lax.axis_size("tm")
                source = (tm_place - (j + 1) + span_count) % span_count
                prev_edge += jnp.where(source == tm_place - 1, there[j, :, -1], 0.0)
                store_before += jnp.where(source < tm_place, jnp.sum(there[j], axis=1), 0.0)
        if iteration == ITERS - 1:
            return (updated, line_dual)
        balance_dual = balance_dual + surplus[0] / UNITS
        previous = jnp.concatenate([prev_edge[:, None], extrap[:, :-1]], axis=1)
        moved = ramp_dual + DUAL_STEP * (extrap - previous) * hour_mask
        ramp_dual = moved - jnp.clip(moved, -DUAL_STEP * ramp[:, None], DUAL_STEP * ramp[:, None])
        running = exact(extrap, forward_table) + store_before[:, None]
        moved = store_dual + DUAL_STEP * storage[:, None] * running
        store_dual = moved - jnp.clip(
            moved, -DUAL_STEP * energy[:, None], DUAL_STEP * energy[:, None]
        )
        generation = updated


def solution(mesh):
    return jax.shard_map(
        on_device,
        mesh=mesh,
        in_specs=(
            P("line", "bus"),
            P("bus", "tm"),
            P(("line", "bus")),
            P(("line", "bus")),
            P(("line", "bus")),
            P(("line", "bus")),
            P("line"),
        ),
        out_specs=(P(("line", "bus"), "tm"), P("line", "tm")),
        check_vma=False,
    )
```
